32 devices in a mesh: dp: 8 (over z, x), tile: 4 (over y, core).
Axes of the slice: x: 2, y: 2, z: 4, core: 2. Of those that a mesh axis runs over, the one named last changes fastest.
Arguments:
- queries: bfloat16 [8, 960, 1536], P('dp', 'tile'), may hold values from -100 to 100
- key_vectors: bfloat16 [8, 960, 1536], P('dp', 'tile'), may hold values from -4 to 4
- value_vectors: bfloat16 [8, 960, 1536], P('dp', 'tile'), may hold values from -6 to 6
- out_weight: bfloat16 [1536, 3072], P('dp', 'tile'), may hold values from -0.15625 to 0.15625
- cotangent: bfloat16 [8, 960, 3072], P('dp', 'tile'), may hold values from -6 to 6
Outputs:
- projected: bfloat16 [8, 960, 3072], P('dp', 'tile')
- query_grad: bfloat16 [8, 960, 1536], P('dp', 'tile')
- key_grad: bfloat16 [8, 960, 1536], P('dp', 'tile')
- value_grad: bfloat16 [8, 960, 1536], P('dp', 'tile')
- weight_grad: float32 [1536, 3072], P('dp', 'tile')
The draws below stay inside these ranges and needn't reach their ends.
All inputs are finite; a program needn't handle non-finite values.
Results may differ from the reference program's by a relative error of at most 0.035.
Values may be sent and summed in bfloat16 or wider, within the bound.
No kernel may reach another device: no remote copies, remote signals or barrier semaphores. Data moves between devices by JAX's collectives and lax.ppermute only.
A program may use at most 128 MiB of HBM per device.

```python
import jax
import jax.numpy as jnp
from jax import lax

D = 3072
HEADS = 12
HEAD = 128
TILE = 120
TILES_DEV = 2
HD = 1536
CLIP_TOK = 960
CLIPS = 8


def key_base(key):
    return jnp.clip(jax.random.normal(key, (CLIPS, CLIP_TOK, HD), jnp.float32), -4.0, 4.0)


def draw_key_vectors(key, part):
    shared = key_base(key)
    return shared.astype(jnp.bfloat16)


def draw_queries(key, part):
    key = jax.random.fold_in(key, 7)
    fresh = jnp.clip(2.0 * jax.random.normal(key, (CLIPS, CLIP_TOK, HD), jnp.float32), -8.0, 8.0)
    return fresh.astype(jnp.bfloat16)


def spiked(entries, key, source, target, parts, factor):
    owner, partner = [(jnp.arange(entries.shape[dim]) // (entries.shape[dim] // parts)).reshape([-1 if axis == dim else 1 for axis in range(entries.ndim)]) for dim in (source, target)]
    chosen = jax.random.permutation(key, parts)[partner]
    strong = (owner == chosen) | (owner == (partner + parts // 2) % parts)
    return jnp.where(strong, factor * entries, entries)


def levels(own_key, shape, cuts, least, high):
    def one(dim, shards_of):
        steps = jax.random.uniform(jax.random.fold_in(jax.random.fold_in(own_key, 6), dim), (shards_of,), jnp.float32, least / len(cuts), high / len(cuts))
        return jnp.repeat(jnp.exp(steps), shape[dim] // shards_of).reshape((-1,) + (1,) * (len(shape) - dim - 1))

    level = one(*cuts[0])
    for cut in cuts[1:]:
        level = level * one(*cut)
    return level


def centred(stream_key, dims, deviation, reach, split=(), dtype=jnp.bfloat16):
    result = jax.random.normal(stream_key, dims, jnp.float32) * deviation
    if len(split) > 0:
        result = levels(stream_key, dims, split, -0.22, 0.18) * result
    return jnp.clip(result, min=-reach, max=reach).astype(dtype)


def heavy_noise(stream_key, dims, scale, reach, split, heavy, dtype=jnp.bfloat16):
    values = scale * jax.random.normal(stream_key, dims, jnp.float32)
    if split:
        values = values * levels(stream_key, dims, split, -0.22, 0.18)
    return jnp.clip(spiked(values, jax.random.fold_in(stream_key, 3), *heavy), -reach, reach).astype(dtype)


def setup_inputs(seed: int = 0) -> dict:
    key_list = jax.random.split(jax.random.key(seed), 6)
    return {
        "queries": draw_queries(jax.random.fold_in(key_list[5], 71), 0),
        "key_vectors": draw_key_vectors(jax.random.fold_in(key_list[5], 71), 0),
        "value_vectors": heavy_noise(key_list[2], (CLIPS, CLIP_TOK, HD), 1.0, 6.0, ((0, 8), (1, 4)), (0, 2, 8, 2.0)),
        "out_weight": centred(key_list[3], (HD, D), HD ** -0.5, 0.15625, ((0, 8), (1, 4))),
        "cotangent": centred(key_list[4], (CLIPS, CLIP_TOK, D), 1.0, 6.0, ((0, 8), (1, 4))),
    }


def half_again(values):
    return lax.optimization_barrier(values.astype(jnp.bfloat16)).astype(jnp.float32)


def windows(tiles):
    zero_tile = jnp.zeros_like(tiles[:1])
    padded = jnp.concatenate([zero_tile, tiles, zero_tile], axis=0)
    return jnp.concatenate([padded[:-2], padded[1:-1], padded[2:]], axis=1)


def collect_keys(contrib):
    tile_total = contrib.shape[0]
    zero_tile = jnp.zeros_like(contrib[:1, 0])
    centre = contrib[:, 1]
    from_after = jnp.concatenate([contrib[1:, 0], zero_tile], axis=0)
    from_before = jnp.concatenate([zero_tile, contrib[:-1, 2]], axis=0)
    tile_index = jnp.arange(tile_total)
    cross_after = ((tile_index + 1) % TILES_DEV == 0)[:, None, None]
    cross_before = (tile_index % TILES_DEV == 0)[:, None, None]
    summed = centre + jnp.where(cross_after, half_again(from_after), from_after)
    summed = summed + jnp.where(cross_before, half_again(from_before), from_before)
    return summed.astype(jnp.bfloat16).reshape(tile_total * TILE, HD)


def clip_pass(clip_queries, clip_keys, clip_values, out_weight, clip_grad):
    tile_total = CLIP_TOK // TILE
    score_scale = HEAD ** -0.5
    query_tiles = clip_queries.astype(jnp.float32).reshape(tile_total, TILE, HEADS, HEAD)
    key_window = windows(clip_keys.astype(jnp.float32).reshape(tile_total, TILE, HEADS, HEAD))
    value_window = windows(clip_values.astype(jnp.float32).reshape(tile_total, TILE, HEADS, HEAD))
    slot_tile = jnp.arange(tile_total)[:, None] - 1 + jnp.arange(3 * TILE)[None, :] // TILE
    visible = (slot_tile >= 0) & (slot_tile < tile_total)
    scores = jnp.einsum('athd,ashd->ahts', query_tiles, key_window) * score_scale
    scores = jnp.where(visible[:, None, None, :], scores, -1e30)
    row_max = jnp.max(scores, axis=-1, keepdims=True)
    expd = jnp.exp(scores - row_max)
    attn_probs = expd / jnp.sum(expd, axis=-1, keepdims=True)
    probs_half = half_again(attn_probs)
    attention = jnp.einsum('ahts,ashd->athd', probs_half, value_window).astype(jnp.bfloat16).reshape(CLIP_TOK, HD)
    projected = jnp.dot(attention, out_weight, preferred_element_type=jnp.float32).astype(jnp.bfloat16)
    grad_attention = jnp.dot(clip_grad, out_weight.T, preferred_element_type=jnp.float32).astype(jnp.bfloat16)
    weight_term = jnp.dot(attention.T, clip_grad, preferred_element_type=jnp.float32)
    grad_tiles = grad_attention.astype(jnp.float32).reshape(tile_total, TILE, HEADS, HEAD)
    attn_tiles = attention.astype(jnp.float32).reshape(tile_total, TILE, HEADS, HEAD)
    row_dots = jnp.sum(grad_tiles * attn_tiles, axis=-1)
    grad_probs = jnp.einsum('athd,ashd->ahts', grad_tiles, value_window)
    grad_scores = half_again(attn_probs * (grad_probs - jnp.transpose(row_dots, (0, 2, 1))[..., None]))
    query_grad = (jnp.einsum('ahts,ashd->athd', grad_scores, key_window) * score_scale).astype(jnp.bfloat16).reshape(CLIP_TOK, HD)
    key_part = (jnp.einsum('ahts,athd->ashd', grad_scores, query_tiles) * score_scale).reshape(tile_total, 3, TILE, HD)
    value_part = jnp.einsum('ahts,athd->ashd', probs_half, grad_tiles).reshape(tile_total, 3, TILE, HD)
    return projected, query_grad, collect_keys(key_part), collect_keys(value_part), weight_term


def reference(queries, key_vectors, value_vectors, out_weight, cotangent):
    def clip_step(running, inputs):
        clip_queries, clip_keys, clip_values, clip_grad = inputs
        proj_out, query_out, key_out, value_out, weight_term = clip_pass(clip_queries, clip_keys, clip_values, out_weight, clip_grad)
        return running + weight_term, (proj_out, query_out, key_out, value_out)

    start_grad = jnp.zeros((HD, D), jnp.float32)
    weight_grad, stacked = lax.scan(clip_step, start_grad, (queries, key_vectors, value_vectors, cotangent))
    projected, query_grad, key_grad, value_grad = stacked
    return (projected, query_grad, key_grad, value_grad, weight_grad)
```

```python
import functools

import jax
import jax.numpy as jnp
from jax import lax
from jax.experimental import pallas as pl
from jax.experimental.pallas import tpu as pltpu
from jax.sharding import PartitionSpec as P

HEADS = 12
HEAD = 128
TILE = 120
GROUP = 3
SCALE = HEAD**-0.5
VMEM = 48 * 1024 * 1024
BF16 = jnp.bfloat16
F32 = jnp.float32


def dot_nn(a, b):
    return lax.dot_general(a, b, (((1,), (0,)), ((), ())), preferred_element_type=F32)


def dot_nt(a, b):
    return lax.dot_general(a, b, (((1,), (1,)), ((), ())), preferred_element_type=F32)


def dot_tn(a, b):
    return lax.dot_general(a, b, (((0,), (0,)), ((), ())), preferred_element_type=F32)


def cost(flops, nbytes, exps=0):
    return pl.CostEstimate(flops=int(flops), bytes_accessed=int(nbytes), transcendentals=int(exps))


def params():
    return pltpu.CompilerParams(vmem_limit_bytes=VMEM)


def whole():
    return pl.BlockSpec(memory_space=pltpu.VMEM)


def anywhere():
    return pl.BlockSpec(memory_space=pl.ANY)


def upper_rows(rows, cols):
    return lax.broadcasted_iota(jnp.int32, (rows, cols), 0) < TILE


def forward_kernel(q_ref, k_ref, v_ref, kl_ref, vl_ref, kr_ref, vr_ref, a_ref, p_ref, ph_ref):
    rows = q_ref.shape[0]
    position = lax.axis_index("tile")
    has_left = position > 0
    has_right = position < lax.axis_size("tile") - 1
    top = upper_rows(rows, TILE)
    seen = (top & has_left) | (jnp.logical_not(top) & has_right)
    for h in range(GROUP):
        at = pl.ds(h * HEAD, HEAD)
        q = q_ref[:, at]
        s = dot_nt(q, k_ref[:, at]) * SCALE
        sh = jnp.where(top, dot_nt(q, kl_ref[:, at]), dot_nt(q, kr_ref[:, at])) * SCALE
        sh = jnp.where(seen, sh, -1e30)
        top_score = jnp.maximum(
            jnp.max(s, axis=-1, keepdims=True), jnp.max(sh, axis=-1, keepdims=True)
        )
        e = jnp.exp(s - top_score)
        eh = jnp.exp(sh - top_score)
        total = jnp.sum(e, axis=-1, keepdims=True) + jnp.sum(eh, axis=-1, keepdims=True)
        inverse = 1.0 / total
        p = (e * inverse).astype(BF16)
        ph = eh * inverse
        p_ref[h] = p
        ph_ref[h] = ph.astype(BF16)
        out = dot_nn(p, v_ref[:, at])
        out += dot_nn(jnp.where(top, ph, 0.0).astype(BF16), vl_ref[:, at])
        out += dot_nn(jnp.where(top, 0.0, ph).astype(BF16), vr_ref[:, at])
        a_ref[:, at] = out.astype(BF16)


def halo_specs(groups, width):
    keys = pl.BlockSpec((TILE, width), lambda g: (0, g))
    values = pl.BlockSpec((TILE, width), lambda g: (0, groups + g))
    return keys, values


def attention_forward(q, k, v, left, right):
    rows, feats = q.shape
    width = GROUP * HEAD
    groups = feats // width
    col = pl.BlockSpec((rows, width), lambda g: (0, g))
    hk, hv = halo_specs(groups, width)
    return pl.pallas_call(
        forward_kernel,
        grid=(groups,),
        in_specs=[col, col, col, hk, hv, hk, hv],
        out_specs=[
            col,
            pl.BlockSpec((GROUP, rows, rows), lambda g: (g, 0, 0)),
            pl.BlockSpec((GROUP, rows, TILE), lambda g: (g, 0, 0)),
        ],
        out_shape=[
            jax.ShapeDtypeStruct((rows, feats), BF16),
            jax.ShapeDtypeStruct((HEADS, rows, rows), BF16),
            jax.ShapeDtypeStruct((HEADS, rows, TILE), BF16),
        ],
        compiler_params=params(),
        cost_estimate=cost(1.4e9, 8e6, 1.4e6),
        name="attention_forward",
    )(q, k, v, left, left, right, right)


def halo_backward_kernel(
    go_ref, gr_ref, a_ref, q_ref, vl_ref, vr_ref, ph_ref, ga_ref, ds_ref, kl_ref, vl_out, kr_ref, vr_out
):
    rows = q_ref.shape[0]
    top = upper_rows(rows, TILE)
    for h in range(GROUP):
        at = pl.ds(h * HEAD, HEAD)
        q = q_ref[:, at]
        ga = (go_ref[:, at] + gr_ref[:, at].astype(F32)).astype(BF16)
        ga_ref[:, at] = ga
        dots = jnp.sum(ga.astype(F32) * a_ref[:, at].astype(F32), axis=-1, keepdims=True)
        dp = jnp.where(top, dot_nt(ga, vl_ref[:, at]), dot_nt(ga, vr_ref[:, at]))
        ph = ph_ref[h].astype(F32)
        ds = ph * (dp - dots)
        ds_ref[h] = ds.astype(BF16)
        kl_ref[:, at] = (dot_tn(jnp.where(top, ds, 0.0).astype(BF16), q) * SCALE).astype(BF16)
        kr_ref[:, at] = (dot_tn(jnp.where(top, 0.0, ds).astype(BF16), q) * SCALE).astype(BF16)
        vl_out[:, at] = dot_tn(jnp.where(top, ph, 0.0).astype(BF16), ga).astype(BF16)
        vr_out[:, at] = dot_tn(jnp.where(top, 0.0, ph).astype(BF16), ga).astype(BF16)


def halo_backward(grad_own, grad_recv, att, q, left, right, probs_halo):
    rows, feats = q.shape
    width = GROUP * HEAD
    groups = feats // width
    col = pl.BlockSpec((rows, width), lambda g: (0, g))
    rim = pl.BlockSpec((TILE, width), lambda g: (0, g))
    _, hv = halo_specs(groups, width)
    heads = pl.BlockSpec((GROUP, rows, TILE), lambda g: (g, 0, 0))
    return pl.pallas_call(
        halo_backward_kernel,
        grid=(groups,),
        in_specs=[col, col, col, col, hv, hv, heads],
        out_specs=[col, heads, rim, rim, rim, rim],
        out_shape=[
            jax.ShapeDtypeStruct((rows, feats), BF16),
            jax.ShapeDtypeStruct((HEADS, rows, TILE), BF16),
        ]
        + [jax.ShapeDtypeStruct((TILE, feats), BF16)] * 4,
        compiler_params=params(),
        cost_estimate=cost(1.0e9, 8e6),
        name="halo_backward",
    )(grad_own, grad_recv, att, q, left, right, probs_halo)


def main_backward_kernel(
    ga_ref, a_ref, q_ref, k_ref, v_ref, kl_ref, kr_ref, p_ref, dsh_ref, dq_ref, dk_ref, dv_ref
):
    rows = q_ref.shape[0]
    top = upper_rows(rows, TILE)
    for h in range(GROUP):
        at = pl.ds(h * HEAD, HEAD)
        q = q_ref[:, at]
        ga = ga_ref[:, at]
        dots = jnp.sum(ga.astype(F32) * a_ref[:, at].astype(F32), axis=-1, keepdims=True)
        p = p_ref[h]
        ds = (p.astype(F32) * (dot_nt(ga, v_ref[:, at]) - dots)).astype(BF16)
        dsh = dsh_ref[h].astype(F32)
        dq = dot_nn(ds, k_ref[:, at])
        dq += dot_nn(jnp.where(top, dsh, 0.0).astype(BF16), kl_ref[:, at])
        dq += dot_nn(jnp.where(top, 0.0, dsh).astype(BF16), kr_ref[:, at])
        dq_ref[:, at] = (dq * SCALE).astype(BF16)
        dk_ref[:, at] = dot_tn(ds, q) * SCALE
        dv_ref[:, at] = dot_tn(p, ga)


def main_backward(ga, att, q, k, v, left, right, probs, ds_halo):
    rows, feats = q.shape
    width = GROUP * HEAD
    groups = feats // width
    col = pl.BlockSpec((rows, width), lambda g: (0, g))
    hk, _ = halo_specs(groups, width)
    return pl.pallas_call(
        main_backward_kernel,
        grid=(groups,),
        in_specs=[
            col,
            col,
            col,
            col,
            col,
            hk,
            hk,
            pl.BlockSpec((GROUP, rows, rows), lambda g: (g, 0, 0)),
            pl.BlockSpec((GROUP, rows, TILE), lambda g: (g, 0, 0)),
        ],
        out_specs=[col, col, col],
        out_shape=[
            jax.ShapeDtypeStruct((rows, feats), BF16),
            jax.ShapeDtypeStruct((rows, feats), F32),
            jax.ShapeDtypeStruct((rows, feats), F32),
        ],
        compiler_params=params(),
        cost_estimate=cost(1.5e9, 1e7),
        name="main_backward",
    )(ga, att, q, k, v, left, right, probs, ds_halo)


def add_rims_body(own_k, own_v, lk, lv, rk, rv, out_k, out_v):
    rows = own_k.shape[0]
    for own, low, high, out in ((own_k, lk, rk, out_k), (own_v, lv, rv, out_v)):
        extra = jnp.concatenate([low[...].astype(F32), high[...].astype(F32)], axis=0)
        out[...] = (own[...] + extra[:rows]).astype(BF16)


def add_rims(dk, dv, lk, lv, rk, rv):
    rows, feats = dk.shape
    width = GROUP * HEAD
    col = pl.BlockSpec((rows, width), lambda g: (0, g))
    rim = pl.BlockSpec((TILE, width), lambda g: (0, g))
    return pl.pallas_call(
        add_rims_body,
        grid=(feats // width,),
        in_specs=[col, col, rim, rim, rim, rim],
        out_specs=[col, col],
        out_shape=[jax.ShapeDtypeStruct((rows, feats), BF16)] * 2,
        compiler_params=params(),
        cost_estimate=cost(1e6, 6e6),
        name="add_rims",
    )(dk, dv, lk, lv, rk, rv)


def grad_attention_kernel(c_ref, w_own, w_other, out_ref, *, sliced):
    place = lax.axis_index("tile")
    core = lax.rem(place, 2)
    half = lax.div(place, 2) if sliced else 0
    width = w_own.shape[1]
    own_at = pl.multiple_of((2 * half + core) * width, 128)
    other_at = pl.multiple_of((2 * half + 1 - core) * width, 128)
    total = dot_nt(c_ref[:, pl.ds(own_at, width)], w_own[...])
    total += dot_nt(c_ref[:, pl.ds(other_at, width)], w_other[...])
    out_ref[...] = total.astype(out_ref.dtype)


def grad_attention_part(cot, w_own, w_other, dtype, sliced):
    rows = cot.shape[0]
    feats, width = w_own.shape
    steps = 4
    block = feats // steps
    wspec = pl.BlockSpec((block, width), lambda g: (g, 0))
    return pl.pallas_call(
        functools.partial(grad_attention_kernel, sliced=sliced),
        grid=(steps,),
        in_specs=[pl.BlockSpec(cot.shape, lambda g: (0, 0)), wspec, wspec],
        out_specs=pl.BlockSpec((rows, block), lambda g: (0, g)),
        out_shape=jax.ShapeDtypeStruct((rows, feats), dtype),
        compiler_params=params(),
        cost_estimate=cost(4 * rows * feats * width, 7e6),
        name="grad_attention_part",
    )(cot, w_own, w_other)


def project_kernel(a_ref, w_own, w_other, out_ref):
    core = lax.rem(lax.axis_index("tile"), 2)
    width = w_own.shape[1]
    a = a_ref[...]
    out_ref[:, pl.ds(pl.multiple_of(core * width, 128), width)] = dot_nn(a, w_own[...]).astype(BF16)
    out_ref[:, pl.ds(pl.multiple_of((1 - core) * width, 128), width)] = dot_nn(
        a, w_other[...]
    ).astype(BF16)


def project_half(att, w_own, w_other):
    rows = att.shape[0]
    feats, width = w_own.shape
    return pl.pallas_call(
        project_kernel,
        in_specs=[whole()] * 3,
        out_specs=whole(),
        out_shape=jax.ShapeDtypeStruct((rows, 2 * width), BF16),
        compiler_params=params(),
        cost_estimate=cost(4 * rows * feats * width, 7e6),
        name="project_half",
    )(att, w_own, w_other)


def project_out_kernel(mine, theirs, out_ref):
    half = lax.div(lax.axis_index("tile"), 2)
    width = mine.shape[1]
    out_ref[:, pl.ds(pl.multiple_of(half * width, 128), width)] = mine[...]
    out_ref[:, pl.ds(pl.multiple_of((1 - half) * width, 128), width)] = theirs[...]


def project_out(mine, theirs):
    rows, width = mine.shape
    return pl.pallas_call(
        project_out_kernel,
        in_specs=[whole()] * 2,
        out_specs=whole(),
        out_shape=jax.ShapeDtypeStruct((rows, 2 * width), BF16),
        compiler_params=params(),
        cost_estimate=cost(1e5, 3e6),
        name="project_out",
    )(mine, theirs)


def assemble_kernel(*refs, places):
    *pieces, out, sems = refs
    pos = lax.axis_index("dp")
    z, x = lax.div(pos, 2), lax.rem(pos, 2)
    rows = pieces[0].shape[0]
    copies = []
    for i, (piece, (shift, flip)) in enumerate(zip(pieces, places)):
        block = 2 * lax.rem(z + 4 - shift, 4) + (1 - x if flip else x)
        start = pl.multiple_of(block * rows, 16)
        copies.append(pltpu.make_async_copy(piece, out.at[pl.ds(start, rows)], sems.at[i]))
    for copy in copies:
        copy.start()
    for copy in copies:
        copy.wait()


def assemble(pieces, places):
    rows, width = pieces[0].shape
    n = len(pieces)
    return pl.pallas_call(
        functools.partial(assemble_kernel, places=places),
        in_specs=[anywhere()] * n,
        out_specs=anywhere(),
        out_shape=jax.ShapeDtypeStruct((n * rows, width), BF16),
        scratch_shapes=[pltpu.SemaphoreType.DMA((n,))],
        compiler_params=params(),
        cost_estimate=cost(0, 5e6),
        name="assemble_weight",
    )(*pieces)


def dp_shift(block, shift, flip):
    route = []
    for z in range(4):
        for x in range(2):
            to = 2 * ((z + shift) % 4) + (1 - x if flip else x)
            route.append((2 * z + x, to))
    return lax.ppermute(block, "dp", route)


def gather_weight(shard):
    if lax.axis_size("dp") != 8:
        return lax.all_gather(shard, "dp", axis=0, tiled=True)
    pieces = {(0, False): shard}
    for shift in (1, 3, 2):
        pieces[shift, False] = dp_shift(shard, shift, False)
    for shift in (0, 1, 3, 2):
        pieces[shift, True] = dp_shift(pieces[shift, False], 0, True)
    places = tuple(pieces)
    return assemble([pieces[p] for p in places], places)


def weight_grad_kernel(a0, a1, a2, a3, c0, c1, c2, c3, keep_ref, send_ref, total, *, shift):
    pos = lax.axis_index("dp")
    z, x = lax.div(pos, 2), lax.rem(pos, 2)
    rows = total.shape[0]
    half = rows // 2
    start = pl.multiple_of(lax.rem(z + shift, 4) * rows, 128)
    acc = dot_tn(a0[:, pl.ds(start, rows)], c0[...])
    acc += dot_tn(a1[:, pl.ds(start, rows)], c1[...])
    acc += dot_tn(a2[:, pl.ds(start, rows)], c2[...])
    acc += dot_tn(a3[:, pl.ds(start, rows)], c3[...])
    total[...] = acc
    keep_ref[...] = total[pl.ds(pl.multiple_of(x * half, 16), half), :]
    send_ref[...] = total[pl.ds(pl.multiple_of((1 - x) * half, 16), half), :].astype(BF16)


def weight_grad_part(atts, cots, shift):
    rows, feats = atts[0].shape
    width = cots[0].shape[1]
    part = feats // 4
    return pl.pallas_call(
        functools.partial(weight_grad_kernel, shift=shift),
        in_specs=[whole()] * 8,
        out_specs=[whole()] * 2,
        out_shape=[
            jax.ShapeDtypeStruct((part // 2, width), F32),
            jax.ShapeDtypeStruct((part // 2, width), BF16),
        ],
        scratch_shapes=[pltpu.VMEM((part, width), F32)],
        compiler_params=params(),
        cost_estimate=cost(8 * rows * part * width, 6e6),
        name="weight_grad_part",
    )(*atts, *cots)


def weight_grad_sum(atts, cots):
    if lax.axis_size("dp") != 8:
        total = sum(dot_tn(a, c) for a, c in zip(atts, cots))
        return lax.psum_scatter(total, "dp", scatter_dimension=0, tiled=True)
    arrived = []
    for shift in (2, 1, 3):
        keep, send = weight_grad_part(atts, cots, shift)
        both = keep + dp_shift(send, 0, True).astype(F32)
        arrived.append(dp_shift(both.astype(BF16), shift, False))
    keep, send = weight_grad_part(atts, cots, 0)
    total = keep + dp_shift(send, 0, True).astype(F32)
    for block in arrived:
        total = total + block.astype(F32)
    return total


def along_tile(block, distance):
    count = lax.axis_size("tile")
    route = [(i, i + distance) for i in range(count) if 0 <= i + distance < count]
    return lax.ppermute(block, "tile", route)


def to_partner(block):
    return lax.ppermute(block, "tile", [(0, 2), (1, 3), (2, 0), (3, 1)])


def to_core(block):
    return lax.ppermute(block, "tile", [(0, 1), (1, 0), (2, 3), (3, 2)])


def shards(queries, key_vectors, value_vectors, out_weight, cotangent):
    q, k, v, cot = queries[0], key_vectors[0], value_vectors[0], cotangent[0]
    tokens, feats = q.shape
    model = cot.shape[1]
    place = lax.axis_index("tile")
    y, core = place // 2, place % 2
    quarter = model // 4

    left = along_tile(jnp.concatenate([k[tokens - TILE :], v[tokens - TILE :]], axis=1), 1)
    right = along_tile(jnp.concatenate([k[:TILE], v[:TILE]], axis=1), -1)
    w_own = gather_weight(out_weight)
    w_other = to_core(w_own)
    cot_partner = to_partner(lax.dynamic_slice_in_dim(cot, (1 - y) * (model // 2), model // 2, axis=1))

    att, probs, probs_halo = attention_forward(q, k, v, left, right)
    att_partner = to_partner(att)

    grad_partner = grad_attention_part(cot_partner, w_own, w_other, BF16, False)
    grad_recv = to_partner(grad_partner)
    grad_own = grad_attention_part(cot, w_own, w_other, F32, True)

    my_at = (2 * y + core) * quarter
    sib_at = (2 * y + 1 - core) * quarter
    c_own = lax.dynamic_slice_in_dim(cot, my_at, quarter, axis=1)
    c_sib = to_core(lax.dynamic_slice_in_dim(cot, sib_at, quarter, axis=1))
    c_par = lax.dynamic_slice_in_dim(cot_partner, core * quarter, quarter, axis=1)
    c_sibpar = to_core(
        lax.dynamic_slice_in_dim(cot_partner, (1 - core) * quarter, quarter, axis=1)
    )
    a_sib = to_core(att)
    a_sibpar = to_core(att_partner)
    weight_grad = weight_grad_sum(
        (att, a_sib, att_partner, a_sibpar), (c_own, c_sib, c_par, c_sibpar)
    )

    proj_partner = project_half(att_partner, w_own, w_other)
    proj_recv = to_partner(proj_partner)
    proj_own = project_half(att, w_own, w_other)
    projected = project_out(proj_own, proj_recv)

    ga, ds_halo, kl, vl, kr, vr = halo_backward(
        grad_own, grad_recv, att, q, left, right, probs_halo
    )
    lk, lv = along_tile(kr, 1), along_tile(vr, 1)
    rk, rv = along_tile(kl, -1), along_tile(vl, -1)
    dq, dk, dv = main_backward(ga, att, q, k, v, left, right, probs, ds_halo)
    dk, dv = add_rims(dk, dv, lk, lv, rk, rv)
    return projected[None], dq[None], dk[None], dv[None], weight_grad


def solution(mesh):
    tokens = P("dp", "tile", None)
    weight = P("dp", "tile")
    return jax.shard_map(
        shards,
        mesh=mesh,
        in_specs=(tokens, tokens, tokens, weight, tokens),
        out_specs=(tokens, tokens, tokens, tokens, weight),
        check_vma=False,
    )
```

```python
import functools

import jax
import jax.numpy as jnp
from jax import lax
from jax.experimental import pallas as pl
from jax.experimental.pallas import tpu as pltpu
from jax.sharding import PartitionSpec as P

HEADS = 12
HEAD = 128
TILE = 120
GROUP = 3
NEAR = (0, 1, 3)
FAR = 2
SCALE = HEAD**-0.5
VMEM = 32 * 1024 * 1024
FIRST = 60 * 1024 * 1024
BF16 = jnp.bfloat16
F32 = jnp.float32


def dot_nn(a, b):
    return lax.dot_general(a, b, (((1,), (0,)), ((), ())), preferred_element_type=F32)


def dot_nt(a, b):
    return lax.dot_general(a, b, (((1,), (1,)), ((), ())), preferred_element_type=F32)


def dot_tn(a, b):
    return lax.dot_general(a, b, (((0,), (0,)), ((), ())), preferred_element_type=F32)


WEIGHT = {}


def cost(name):
    return pl.CostEstimate(
        flops=int(WEIGHT.get(name, 3e10)), bytes_accessed=int(1e10), transcendentals=0
    )


def whole():
    return pl.BlockSpec(memory_space=pltpu.VMEM)


def anywhere():
    return pl.BlockSpec(memory_space=pl.ANY)


def shape(dims, dtype=BF16):
    return jax.ShapeDtypeStruct(dims, dtype)


def run(kernel, args, in_specs, out_specs, out_shape, name, after=(), grid=(), limit=VMEM, **extra):
    count, skipped = len(args), len(after)

    def body(*refs):
        kernel(*refs[:count], *refs[count + skipped :])

    return pl.pallas_call(
        body,
        grid=grid,
        in_specs=list(in_specs) + [anywhere()] * skipped,
        out_specs=out_specs,
        out_shape=out_shape,
        compiler_params=pltpu.CompilerParams(vmem_limit_bytes=limit),
        cost_estimate=cost(name),
        name=name,
        **extra,
    )(*args, *after)


def relay(block, after):
    def body(*refs):
        pass

    return pl.pallas_call(
        body,
        in_specs=[anywhere()] * (1 + len(after)),
        out_specs=anywhere(),
        out_shape=shape(block.shape, block.dtype),
        input_output_aliases={0: 0},
        cost_estimate=cost("relay"),
        name="relay",
    )(block, *after)


def facing_rows(rows, cols):
    y, core = place()
    top = lax.broadcasted_iota(jnp.int32, (rows, cols), 0) < TILE
    return top == (core == 0)


def place():
    tile = lax.axis_index("tile")
    return lax.div(tile, 2), lax.rem(tile, 2)


def columns(start, width):
    return pl.ds(pl.multiple_of(start, 128), width)


def rows_at(start, count):
    return pl.ds(pl.multiple_of(start, 16), count)


def forward_kernel(q_ref, k_ref, v_ref, kl_ref, vl_ref, kr_ref, vr_ref, a_ref, p_ref, ph_ref):
    rows = q_ref.shape[0]
    y, core = place()
    facing = facing_rows(rows, TILE)
    seen = jnp.logical_not(facing) | (y != core)
    for h in range(GROUP):
        at = pl.ds(h * HEAD, HEAD)
        q = q_ref[:, at]
        s = dot_nt(q, k_ref[:, at]) * SCALE
        sh = jnp.where(facing, dot_nt(q, kl_ref[:, at]), dot_nt(q, kr_ref[:, at])) * SCALE
        sh = jnp.where(seen, sh, -1e30)
        top_score = jnp.maximum(
            jnp.max(s, axis=-1, keepdims=True), jnp.max(sh, axis=-1, keepdims=True)
        )
        e = jnp.exp(s - top_score)
        eh = jnp.exp(sh - top_score)
        total = jnp.sum(e, axis=-1, keepdims=True) + jnp.sum(eh, axis=-1, keepdims=True)
        inverse = 1.0 / total
        p = (e * inverse).astype(BF16)
        ph = eh * inverse
        p_ref[h] = p
        ph_ref[h] = ph.astype(BF16)
        out = dot_nn(p, v_ref[:, at])
        out += dot_nn(jnp.where(facing, ph, 0.0).astype(BF16), vl_ref[:, at])
        out += dot_nn(jnp.where(facing, 0.0, ph).astype(BF16), vr_ref[:, at])
        a_ref[:, at] = out.astype(BF16)


def attention_specs(rows, feats):
    width = GROUP * HEAD
    groups = feats // width
    col = pl.BlockSpec((rows, width), lambda g: (0, g))
    halo_keys = pl.BlockSpec((TILE, width), lambda g: (0, g))
    halo_values = pl.BlockSpec((TILE, width), lambda g: (0, groups + g))
    own = pl.BlockSpec((GROUP, rows, rows), lambda g: (g, 0, 0))
    halo = pl.BlockSpec((GROUP, rows, TILE), lambda g: (g, 0, 0))
    return groups, col, halo_keys, halo_values, own, halo


def attention_forward(q, k, v, halo_chip, halo_core, after):
    rows, feats = q.shape
    groups, col, hk, hv, own, halo = attention_specs(rows, feats)
    return run(
        forward_kernel,
        (q, k, v, halo_chip, halo_chip, halo_core, halo_core),
        [col, col, col, hk, hv, hk, hv],
        [col, own, halo],
        [shape((rows, feats)), shape((HEADS, rows, rows)), shape((HEADS, rows, TILE))],
        "attention_forward",
        after,
        (groups,),
    )


def halo_backward_kernel(
    ga_ref, a_ref, q_ref, vl_ref, vr_ref, ph_ref, ds_ref, chip_ref, core_ref
):
    rows = q_ref.shape[0]
    feats = chip_ref.shape[1] // 2
    facing = facing_rows(rows, TILE)
    first = pl.program_id(0) * (GROUP * HEAD)
    for h in range(GROUP):
        at = pl.ds(h * HEAD, HEAD)
        to_key = columns(first + h * HEAD, HEAD)
        to_value = columns(first + feats + h * HEAD, HEAD)
        q = q_ref[:, at]
        ga = ga_ref[:, at]
        dots = jnp.sum(ga.astype(F32) * a_ref[:, at].astype(F32), axis=-1, keepdims=True)
        dp = jnp.where(facing, dot_nt(ga, vl_ref[:, at]), dot_nt(ga, vr_ref[:, at]))
        ph = ph_ref[h].astype(F32)
        ds = ph * (dp - dots)
        ds_ref[h] = ds.astype(BF16)
        chip_ref[:, to_key] = (dot_tn(jnp.where(facing, ds, 0.0).astype(BF16), q) * SCALE).astype(BF16)
        core_ref[:, to_key] = (dot_tn(jnp.where(facing, 0.0, ds).astype(BF16), q) * SCALE).astype(BF16)
        chip_ref[:, to_value] = dot_tn(jnp.where(facing, ph, 0.0).astype(BF16), ga).astype(BF16)
        core_ref[:, to_value] = dot_tn(jnp.where(facing, 0.0, ph).astype(BF16), ga).astype(BF16)


def halo_backward(ga, att, q, halo_chip, halo_core, probs_halo):
    rows, feats = q.shape
    groups, col, hk, hv, own, halo = attention_specs(rows, feats)
    rim = pl.BlockSpec((TILE, 2 * feats), lambda g: (0, 0))
    return run(
        halo_backward_kernel,
        (ga, att, q, halo_chip, halo_core, probs_halo),
        [col, col, col, hv, hv, halo],
        [halo, rim, rim],
        [shape((HEADS, rows, TILE))] + [shape((TILE, 2 * feats))] * 2,
        "halo_backward",
        (),
        (groups,),
    )


def main_backward_kernel(
    ga_ref, a_ref, q_ref, k_ref, v_ref, kl_ref, kr_ref, p_ref, dsh_ref, dq_ref, dk_ref, dv_ref
):
    rows = q_ref.shape[0]
    facing = facing_rows(rows, TILE)
    for h in range(GROUP):
        at = pl.ds(h * HEAD, HEAD)
        q = q_ref[:, at]
        ga = ga_ref[:, at]
        dots = jnp.sum(ga.astype(F32) * a_ref[:, at].astype(F32), axis=-1, keepdims=True)
        p = p_ref[h]
        ds = (p.astype(F32) * (dot_nt(ga, v_ref[:, at]) - dots)).astype(BF16)
        dsh = dsh_ref[h].astype(F32)
        dq = dot_nn(ds, k_ref[:, at])
        dq += dot_nn(jnp.where(facing, dsh, 0.0).astype(BF16), kl_ref[:, at])
        dq += dot_nn(jnp.where(facing, 0.0, dsh).astype(BF16), kr_ref[:, at])
        dq_ref[:, at] = (dq * SCALE).astype(BF16)
        dk_ref[:, at] = dot_tn(ds, q) * SCALE
        dv_ref[:, at] = dot_tn(p, ga)


def main_backward(ga, att, q, k, v, halo_chip, halo_core, probs, ds_halo, after):
    rows, feats = q.shape
    groups, col, hk, hv, own, halo = attention_specs(rows, feats)
    return run(
        main_backward_kernel,
        (ga, att, q, k, v, halo_chip, halo_core, probs, ds_halo),
        [col, col, col, col, col, hk, hk, own, halo],
        [col, col, col],
        [shape((rows, feats)), shape((rows, feats), F32), shape((rows, feats), F32)],
        "main_backward",
        after,
        (groups,),
    )


def add_rims_kernel(own_k, own_v, lk, lv, rk, rv, out_k, out_v):
    y, core = place()
    for own, chip, other, out in ((own_k, lk, rk, out_k), (own_v, lv, rv, out_v)):
        far, near = chip[...].astype(F32), other[...].astype(F32)
        low, high = jnp.where(core == 0, far, near), jnp.where(core == 0, near, far)
        extra = jnp.concatenate([low, high], axis=0)
        out[...] = (own[...] + extra).astype(BF16)


def add_rims(dk, dv, from_chip, from_core):
    rows, feats = dk.shape
    groups, col, hk, hv, own, halo = attention_specs(rows, feats)
    return run(
        add_rims_kernel,
        (dk, dv, from_chip, from_chip, from_core, from_core),
        [col, col, hk, hv, hk, hv],
        [col, col],
        [shape((rows, feats))] * 2,
        "add_rims",
        (),
        (groups,),
    )


def first_sends_kernel(k_ref, v_ref, w_ref, c_ref, chip_ref, core_ref, shard_ref, half_ref, held, sems):
    y, core = place()
    rows, feats = k_ref.shape
    parts = 4
    part = feats // parts
    copies = []
    for i, source in enumerate((k_ref, v_ref)):
        for j in range(parts):
            at = pl.ds(j * part, part)
            copies.append((source.at[:, at], held.at[i, :, at]))
    copies.append((w_ref, shard_ref))
    for j in range(parts):
        at = columns((1 - y) * feats + j * part, part)
        copies.append((c_ref.at[:, at], half_ref.at[:, pl.ds(j * part, part)]))
    copies = [pltpu.make_async_copy(*ends, sems.at[i]) for i, ends in enumerate(copies)]
    for copy in copies:
        copy.start()
    for copy in copies:
        copy.wait()
    for i in range(2):
        at = pl.ds(i * feats, feats)
        low, high = held[i, :TILE], held[i, rows - TILE :]
        chip_ref[:, at] = jnp.where(core == 0, low, high)
        core_ref[:, at] = jnp.where(core == 0, high, low)


def first_sends(k, v, w, cot):
    rows, feats = k.shape
    return run(
        first_sends_kernel,
        (k, v, w, cot),
        [pl.BlockSpec(memory_space=pltpu.HBM)] * 4,
        [whole()] * 4,
        [shape((TILE, 2 * feats))] * 2 + [shape(w.shape), shape((rows, cot.shape[1] // 2))],
        "first_sends",
        limit=FIRST,
        scratch_shapes=[pltpu.VMEM((2, rows, feats), BF16), pltpu.SemaphoreType.DMA((13,))],
    )


def quarters_for_core_kernel(cot_ref, partner_ref, out_ref):
    y, core = place()
    rows, width = out_ref.shape[0] // 2, out_ref.shape[1]
    out_ref[:rows] = cot_ref[:, columns((2 * y + 1 - core) * width, width)]
    out_ref[rows:] = partner_ref[:, columns((1 - core) * width, width)]


def quarters_for_core(cot, cot_partner, after):
    rows, model = cot.shape
    return run(
        quarters_for_core_kernel,
        (cot, cot_partner),
        [whole()] * 2,
        whole(),
        shape((2 * rows, model // 4)),
        "quarters_for_core",
        after,
    )


def block_at(shift):
    if not is_grid():
        return shift
    return lax.rem(lax.div(lax.axis_index("dp"), 2) + 4 - shift, 4)


def lay(pair, block):
    x = lax.rem(lax.axis_index("dp"), 2) if is_grid() else 0
    rows = pair[0].shape[0]
    block[rows_at(x * rows, rows), :] = pair[0][...]
    block[rows_at((1 - x) * rows, rows), :] = pair[1][...]


def half_product(c_ref, w_own, w_other, out_ref, sliced):
    y, core = place()
    half = y if sliced else 0
    width = w_own.shape[1]
    total = dot_nt(c_ref[:, columns((2 * half + core) * width, width)], w_own[...])
    total += dot_nt(c_ref[:, columns((2 * half + 1 - core) * width, width)], w_other[...])
    out_ref[...] = total.astype(out_ref.dtype)


def near_kernel(c_ref, w_own, w_other, out_ref, *, sliced):
    half_product(c_ref, w_own, w_other, out_ref, sliced)


def far_kernel(c_ref, own0, own1, other0, other1, out_ref, w_own, w_other, *, sliced):
    lay((own0, own1), w_own)
    lay((other0, other1), w_other)
    half_product(c_ref, w_own, w_other, out_ref, sliced)


def grad_attention_near(cot, near, dtype, sliced, after):
    rows = cot.shape[0]
    return run(
        functools.partial(near_kernel, sliced=sliced),
        (cot, *near),
        [whole()] * 3,
        whole(),
        shape((rows, near[0].shape[0]), dtype),
        "grad_attention_near",
        after,
    )


def grad_attention_far(cot, far, dtype, sliced, after):
    rows = cot.shape[0]
    feats, width = 2 * far[0].shape[0], far[0].shape[1]
    return run(
        functools.partial(far_kernel, sliced=sliced),
        (cot, *far),
        [whole()] * 5,
        whole(),
        shape((rows, feats), dtype),
        "grad_attention_far",
        after,
        scratch_shapes=[pltpu.VMEM((feats, width), BF16)] * 2,
    )


def merge_kernel(own_near, own_far, recv_near, recv_far, out_ref):
    rows, width = own_far.shape
    for i, shift in enumerate((*NEAR, FAR)):
        own, recv = (own_near, recv_near) if i < 3 else (own_far, recv_far)
        at = pl.ds(i * width if i < 3 else 0, width)
        total = own[:, at] + recv[:, at].astype(F32)
        out_ref[:, columns(block_at(shift) * width, width)] = total.astype(BF16)


def merge(own_near, own_far, recv_near, recv_far, after):
    rows, width = own_far.shape
    return run(
        merge_kernel,
        (own_near, own_far, recv_near, recv_far),
        [whole()] * 4,
        whole(),
        shape((rows, 4 * width)),
        "merge",
        after,
    )


def project_kernel(
    a_ref, near_own, near_other, own0, own1, other0, other1, out_ref, far_own, far_other
):
    y, core = place()
    rows, width = far_own.shape
    lay((own0, own1), far_own)
    lay((other0, other1), far_other)
    for quarter, near, far in ((core, near_own, far_own), (1 - core, near_other, far_other)):
        total = dot_nn(a_ref[:, columns(block_at(FAR) * rows, rows)], far[...])
        for i, shift in enumerate(NEAR):
            a = a_ref[:, columns(block_at(shift) * rows, rows)]
            total += dot_nn(a, near[i * rows : (i + 1) * rows])
        out_ref[:, columns(quarter * width, width)] = total.astype(BF16)


def project_half(att, near, far, after):
    rows = att.shape[0]
    feats, width = 2 * far[0].shape[0], far[0].shape[1]
    return run(
        project_kernel,
        (att, *near, *far),
        [whole()] * 7,
        whole(),
        shape((rows, 2 * width)),
        "project_half",
        after,
        scratch_shapes=[pltpu.VMEM((feats, width), BF16)] * 2,
    )


def join_halves_kernel(mine, theirs, out_ref):
    y, core = place()
    width = mine.shape[1]
    out_ref[:, columns(y * width, width)] = mine[...]
    out_ref[:, columns((1 - y) * width, width)] = theirs[...]


def join_halves(mine, theirs):
    rows, width = mine.shape
    return run(
        join_halves_kernel,
        (mine, theirs),
        [whole()] * 2,
        whole(),
        shape((rows, 2 * width)),
        "join_halves",
    )


def assemble_kernel(*refs):
    *pieces, out, sems = refs
    x = lax.rem(lax.axis_index("dp"), 2)
    rows = pieces[0].shape[0]
    copies = []
    for i, piece in enumerate(pieces):
        block = 2 * (i // 2) + (x if i % 2 == 0 else 1 - x)
        copies.append(pltpu.make_async_copy(piece, out.at[rows_at(block * rows, rows)], sems.at[i]))
    for copy in copies:
        copy.start()
    for copy in copies:
        copy.wait()


def assemble(pieces, after):
    rows, width = pieces[0].shape
    n = len(pieces)
    return run(
        assemble_kernel,
        pieces,
        [anywhere()] * n,
        whole(),
        shape((n * rows, width)),
        "assemble_weight",
        after,
        scratch_shapes=[pltpu.SemaphoreType.DMA((n,))],
    )


def along_z(block, shift):
    return lax.ppermute(
        block, "dp", [(2 * z + x, 2 * ((z + shift) % 4) + x) for z in range(4) for x in range(2)]
    )


def across_x(block):
    return lax.ppermute(block, "dp", [(i, i ^ 1) for i in range(8)])


def is_grid():
    return lax.axis_size("dp") == 8


def weight_grad_kernel(
    a_own, a_par, a_sib, a_sibpar, c_own, c_par, c_sib, c_sibpar, *outs_and_total
):
    *outs, total = outs_and_total
    x = lax.rem(lax.axis_index("dp"), 2)
    step = pl.program_id(0)
    half = total.shape[0] // 2
    acc = dot_tn(a_own[...], c_own[...])
    acc += dot_tn(a_par[...], c_par[...])
    acc += dot_tn(a_sib[...], c_sib[...])
    acc += dot_tn(a_sibpar[...], c_sibpar[...])
    total[...] = acc
    keeps, sends = outs[:3], outs[3:]
    for at, (part, row) in enumerate(((0, 0), (1, 0), (1, half), (2, 0))):

        @pl.when(step == at)
        def _():
            keeps[part][row : row + half] = total[rows_at(x * half, half), :]
            sends[part][row : row + half] = total[rows_at((1 - x) * half, half), :].astype(BF16)


def weight_grad_parts(operands, after):
    a_own, a_par, a_sib, a_sibpar, cot, cot_par, c_sib = operands
    tokens, feats = a_own.shape
    width = cot.shape[1] // 4
    part = feats // 4

    def rows_of(g):
        shift = jnp.where(g == 0, 2, jnp.where(g == 1, 1, jnp.where(g == 2, 3, 0)))
        return lax.rem(lax.div(lax.axis_index("dp"), 2) + shift, 4)

    a_spec = pl.BlockSpec((tokens, part), lambda g: (0, rows_of(g)))
    c_specs = [
        pl.BlockSpec((tokens, width), lambda g: (0, lax.axis_index("tile"))),
        pl.BlockSpec((tokens, width), lambda g: (0, lax.rem(lax.axis_index("tile"), 2))),
        pl.BlockSpec((tokens, width), lambda g: (0, 0)),
        pl.BlockSpec((tokens, width), lambda g: (1, 0)),
    ]
    dims = [(part // 2, width), (part, width), (part // 2, width)]
    return run(
        weight_grad_kernel,
        (a_own, a_par, a_sib, a_sibpar, cot, cot_par, c_sib, c_sib),
        [a_spec] * 4 + c_specs,
        [pl.BlockSpec(d, lambda g: (0, 0)) for d in dims * 2],
        [shape(d, F32) for d in dims] + [shape(d) for d in dims],
        "weight_grad_parts",
        after,
        (4,),
        scratch_shapes=[pltpu.VMEM((part, width), F32)],
    )


def weight_grad_sum(operands, after):
    if not is_grid():
        a_own, a_par, a_sib, a_sibpar, cot, cot_par, c_sib = operands
        y, core = place()
        tokens, width = c_sib.shape[0] // 2, c_sib.shape[1]
        c_own = lax.dynamic_slice_in_dim(cot, (2 * y + core) * width, width, axis=1)
        c_par = lax.dynamic_slice_in_dim(cot_par, core * width, width, axis=1)
        total = dot_tn(a_own, c_own) + dot_tn(a_par, c_par)
        total += dot_tn(a_sib, c_sib[:tokens]) + dot_tn(a_sibpar, c_sib[tokens:])
        return lax.psum_scatter(total, "dp", scatter_dimension=0, tiled=True)
    parts = weight_grad_parts(operands, after)
    return [(keep, across_x(send)) for keep, send in zip(parts[:3], parts[3:])]


def add_kernel(*refs):
    *terms, out = refs
    total = terms[0][...].astype(F32)
    for term in terms[1:]:
        total += term[...].astype(F32)
    out[...] = total.astype(out.dtype)


def add(terms, dtype, after=()):
    return run(
        add_kernel,
        terms,
        [whole()] * len(terms),
        whole(),
        shape(terms[0].shape, dtype),
        "add",
        after,
    )


def split_add_kernel(keep, recv, one, three):
    half = one.shape[0]
    one[...] = keep[:half] + recv[:half].astype(F32)
    three[...] = (keep[half:] + recv[half:].astype(F32)).astype(BF16)


def split_add(keep, recv, after=()):
    dims = (keep.shape[0] // 2, keep.shape[1])
    return run(
        split_add_kernel,
        (keep, recv),
        [whole()] * 2,
        [whole()] * 2,
        [shape(dims, F32), shape(dims)],
        "split_add",
        after,
    )


def between_chips(block):
    return lax.ppermute(block, "tile", [(1, 2), (2, 1)])


def to_partner(block):
    return lax.ppermute(block, "tile", [(0, 2), (1, 3), (2, 0), (3, 1)])


def to_core(block):
    return lax.ppermute(block, "tile", [(0, 1), (1, 0), (2, 3), (3, 2)])


def shards(queries, key_vectors, value_vectors, out_weight, cotangent):
    q, k, v, cot = queries[0], key_vectors[0], value_vectors[0], cotangent[0]
    tokens = q.shape[0]
    y, core = place()

    rim_chip, rim_core, shard, cot_send = first_sends(k, v, out_weight, cot)
    halo_chip, halo_core = between_chips(rim_chip), to_core(rim_core)
    if is_grid():
        z1, z3 = along_z(shard, 1), along_z(shard, 3)
        x0 = across_x(shard)
    cot_partner = to_partner(cot_send)
    att, probs, probs_halo = attention_forward(q, k, v, halo_chip, halo_core, ())
    att_partner = to_partner(att)
    att_core = to_core(att)
    if is_grid():
        z1 = relay(z1, (att,))
        z3 = relay(z3, (z1,))
        z2 = relay(along_z(z1, 1), (z3,))
        near_own = assemble(
            (shard, x0, z1, across_x(z1), z3, across_x(z3)), (att, cot_partner)
        )
        far_own = (z2, across_x(z2))
    else:
        w_own = lax.all_gather(out_weight, "dp", axis=0, tiled=True)
        cut = w_own.shape[0] * 3 // 4
        near_own = w_own[:cut]
        far_own = (w_own[cut : cut + cut // 6], w_own[cut + cut // 6 :])
    near = (near_own, to_core(near_own))
    far = (*far_own, to_core(far_own[0]), to_core(far_own[1]))
    cot_send_core = quarters_for_core(cot, cot_partner, ())
    cot_core = to_core(cot_send_core)

    send_near = grad_attention_near(cot_partner, near, BF16, False, (cot_send_core,))
    recv_near = to_partner(send_near)
    send_far = grad_attention_far(cot_partner, far, BF16, False, (send_near,))
    recv_far = to_partner(send_far)

    att_partner = relay(att_partner, (send_far,))
    att_core_partner = to_core(att_partner)
    mine_near = grad_attention_near(cot, near, F32, True, (send_far,))
    parts = weight_grad_sum(
        (att, att_partner, att_core, att_core_partner, cot, cot_partner, cot_core), (mine_near,)
    )
    grid = is_grid()
    mine_far = grad_attention_far(
        cot, far, F32, True, (mine_near, parts[2][0]) if grid else (mine_near,)
    )
    if grid:
        far_sum = add(parts[0], BF16, (mine_far,))
        from_two = along_z(far_sum, 1)
    proj_partner = project_half(att_partner, near, far, (far_sum,) if grid else (mine_far,))
    proj_recv = to_partner(proj_partner)

    ga = merge(mine_near, mine_far, recv_near, recv_far, (far_sum,) if grid else ())
    ds_halo, back_chip, back_core = halo_backward(ga, att, q, halo_chip, halo_core, probs_halo)
    from_chip, from_core = between_chips(back_chip), to_core(back_core)
    if grid:
        one, three = split_add(*parts[1], (ds_halo,))
        from_three = along_z(three, 3)
        one_sum = add((one, from_two), BF16, (three,))
        from_one = along_z(one_sum, 1)
    proj_own = project_half(att, near, far, (one_sum,) if grid else (proj_partner,))
    dq, dk, dv = main_backward(
        ga, att, q, k, v, halo_chip, halo_core, probs, ds_halo, (proj_own,)
    )
    projected = join_halves(proj_own, proj_recv)
    dk, dv = add_rims(dk, dv, from_chip, from_core)
    weight_grad = add((*parts[2], from_three, from_one), F32) if grid else parts
    return projected[None], dq[None], dk[None], dv[None], weight_grad


def solution(mesh):
    tokens = P("dp", "tile", None)
    weight = P("dp", "tile")
    return jax.shard_map(
        shards,
        mesh=mesh,
        in_specs=(tokens, tokens, tokens, weight, tokens),
        out_specs=(tokens, tokens, tokens, tokens, weight),
        check_vma=False,
    )
```

```python
import functools

import jax
import jax.numpy as jnp
from jax import lax
from jax.experimental import pallas as pl
from jax.experimental.pallas import tpu as pltpu
from jax.sharding import PartitionSpec as P

HEADS = 12
HEAD = 128
TILE = 120
GROUP = 3
NEAR = (0, 1, 3)
FAR = 2
SCALE = HEAD**-0.5
VMEM = 32 * 1024 * 1024
FIRST = 60 * 1024 * 1024
BF16 = jnp.bfloat16
F32 = jnp.float32


def dot_nn(a, b):
    return lax.dot_general(a, b, (((1,), (0,)), ((), ())), preferred_element_type=F32)


def dot_nt(a, b):
    return lax.dot_general(a, b, (((1,), (1,)), ((), ())), preferred_element_type=F32)


def dot_tn(a, b):
    return lax.dot_general(a, b, (((0,), (0,)), ((), ())), preferred_element_type=F32)


WEIGHT = {}


def cost(name):
    return pl.CostEstimate(
        flops=int(WEIGHT.get(name, 3e10)), bytes_accessed=int(1e10), transcendentals=0
    )


def whole():
    return pl.BlockSpec(memory_space=pltpu.VMEM)


def anywhere():
    return pl.BlockSpec(memory_space=pl.ANY)


def shape(dims, dtype=BF16):
    return jax.ShapeDtypeStruct(dims, dtype)


def run(kernel, args, in_specs, out_specs, out_shape, name, after=(), grid=(), limit=VMEM, **extra):
    count, skipped = len(args), len(after)

    def body(*refs):
        kernel(*refs[:count], *refs[count + skipped :])

    return pl.pallas_call(
        body,
        grid=grid,
        in_specs=list(in_specs) + [anywhere()] * skipped,
        out_specs=out_specs,
        out_shape=out_shape,
        compiler_params=pltpu.CompilerParams(vmem_limit_bytes=limit),
        cost_estimate=cost(name),
        name=name,
        **extra,
    )(*args, *after)


def relay(block, after):
    def body(*refs):
        pass

    return pl.pallas_call(
        body,
        in_specs=[anywhere()] * (1 + len(after)),
        out_specs=anywhere(),
        out_shape=shape(block.shape, block.dtype),
        input_output_aliases={0: 0},
        cost_estimate=cost("relay"),
        name="relay",
    )(block, *after)


def facing_rows(rows, cols):
    y, core = place()
    top = lax.broadcasted_iota(jnp.int32, (rows, cols), 0) < TILE
    return top == (core == 0)


def place():
    tile = lax.axis_index("tile")
    return lax.div(tile, 2), lax.rem(tile, 2)


def columns(start, width):
    return pl.ds(pl.multiple_of(start, 128), width)


def rows_at(start, count):
    return pl.ds(pl.multiple_of(start, 16), count)


def forward_kernel(q_ref, k_ref, v_ref, kl_ref, vl_ref, kr_ref, vr_ref, a_ref, p_ref, ph_ref):
    rows = q_ref.shape[0]
    y, core = place()
    facing = facing_rows(rows, TILE)
    seen = jnp.logical_not(facing) | (y != core)
    for h in range(GROUP):
        at = pl.ds(h * HEAD, HEAD)
        q = q_ref[:, at]
        s = dot_nt(q, k_ref[:, at]) * SCALE
        sh = jnp.where(facing, dot_nt(q, kl_ref[:, at]), dot_nt(q, kr_ref[:, at])) * SCALE
        sh = jnp.where(seen, sh, -1e30)
        top_score = jnp.maximum(
            jnp.max(s, axis=-1, keepdims=True), jnp.max(sh, axis=-1, keepdims=True)
        )
        e = jnp.exp(s - top_score)
        eh = jnp.exp(sh - top_score)
        total = jnp.sum(e, axis=-1, keepdims=True) + jnp.sum(eh, axis=-1, keepdims=True)
        inverse = 1.0 / total
        p = (e * inverse).astype(BF16)
        ph = eh * inverse
        p_ref[h] = p
        ph_ref[h] = ph.astype(BF16)
        out = dot_nn(p, v_ref[:, at])
        out += dot_nn(jnp.where(facing, ph, 0.0).astype(BF16), vl_ref[:, at])
        out += dot_nn(jnp.where(facing, 0.0, ph).astype(BF16), vr_ref[:, at])
        a_ref[:, at] = out.astype(BF16)


def attention_specs(rows, feats):
    width = GROUP * HEAD
    groups = feats // width
    col = pl.BlockSpec((rows, width), lambda g: (0, g))
    halo_keys = pl.BlockSpec((TILE, width), lambda g: (0, g))
    halo_values = pl.BlockSpec((TILE, width), lambda g: (0, groups + g))
    own = pl.BlockSpec((GROUP, rows, rows), lambda g: (g, 0, 0))
    halo = pl.BlockSpec((GROUP, rows, TILE), lambda g: (g, 0, 0))
    return groups, col, halo_keys, halo_values, own, halo


def attention_forward(q, k, v, halo_chip, halo_core, after):
    rows, feats = q.shape
    groups, col, hk, hv, own, halo = attention_specs(rows, feats)
    return run(
        forward_kernel,
        (q, k, v, halo_chip, halo_chip, halo_core, halo_core),
        [col, col, col, hk, hv, hk, hv],
        [col, own, halo],
        [
            shape((rows, feats)),
            pltpu.HBM((HEADS, rows, rows), BF16),
            pltpu.HBM((HEADS, rows, TILE), BF16),
        ],
        "attention_forward",
        after,
        (groups,),
    )


def halo_backward_kernel(
    ga_ref, a_ref, q_ref, vl_ref, vr_ref, ph_ref, ds_ref, chip_ref, core_ref
):
    rows = q_ref.shape[0]
    feats = chip_ref.shape[1] // 2
    facing = facing_rows(rows, TILE)
    first = pl.program_id(0) * (GROUP * HEAD)
    for h in range(GROUP):
        at = pl.ds(h * HEAD, HEAD)
        to_key = columns(first + h * HEAD, HEAD)
        to_value = columns(first + feats + h * HEAD, HEAD)
        q = q_ref[:, at]
        ga = ga_ref[:, at]
        dots = jnp.sum(ga.astype(F32) * a_ref[:, at].astype(F32), axis=-1, keepdims=True)
        dp = jnp.where(facing, dot_nt(ga, vl_ref[:, at]), dot_nt(ga, vr_ref[:, at]))
        ph = ph_ref[h].astype(F32)
        ds = ph * (dp - dots)
        ds_ref[h] = ds.astype(BF16)
        chip_ref[:, to_key] = (dot_tn(jnp.where(facing, ds, 0.0).astype(BF16), q) * SCALE).astype(BF16)
        core_ref[:, to_key] = (dot_tn(jnp.where(facing, 0.0, ds).astype(BF16), q) * SCALE).astype(BF16)
        chip_ref[:, to_value] = dot_tn(jnp.where(facing, ph, 0.0).astype(BF16), ga).astype(BF16)
        core_ref[:, to_value] = dot_tn(jnp.where(facing, 0.0, ph).astype(BF16), ga).astype(BF16)


def halo_backward(ga, att, q, halo_chip, halo_core, probs_halo):
    rows, feats = q.shape
    groups, col, hk, hv, own, halo = attention_specs(rows, feats)
    rim = pl.BlockSpec((TILE, 2 * feats), lambda g: (0, 0))
    return run(
        halo_backward_kernel,
        (ga, att, q, halo_chip, halo_core, probs_halo),
        [col, col, col, hv, hv, halo],
        [halo, rim, rim],
        [shape((HEADS, rows, TILE))] + [shape((TILE, 2 * feats))] * 2,
        "halo_backward",
        (),
        (groups,),
    )


def main_backward_kernel(
    ga_ref,
    a_ref,
    q_ref,
    k_ref,
    v_ref,
    kl_ref,
    kr_ref,
    p_ref,
    dsh_ref,
    chip_k,
    chip_v,
    core_k,
    core_v,
    dq_ref,
    dk_ref,
    dv_ref,
):
    rows = q_ref.shape[0]
    y, core = place()
    facing = facing_rows(rows, TILE)

    def from_others(chip, other, at):
        far, near = chip[:, at].astype(F32), other[:, at].astype(F32)
        low, high = jnp.where(core == 0, far, near), jnp.where(core == 0, near, far)
        return jnp.concatenate([low, high], axis=0)

    for h in range(GROUP):
        at = pl.ds(h * HEAD, HEAD)
        q = q_ref[:, at]
        ga = ga_ref[:, at]
        dots = jnp.sum(ga.astype(F32) * a_ref[:, at].astype(F32), axis=-1, keepdims=True)
        p = p_ref[h]
        ds = (p.astype(F32) * (dot_nt(ga, v_ref[:, at]) - dots)).astype(BF16)
        dsh = dsh_ref[h].astype(F32)
        dq = dot_nn(ds, k_ref[:, at])
        dq += dot_nn(jnp.where(facing, dsh, 0.0).astype(BF16), kl_ref[:, at])
        dq += dot_nn(jnp.where(facing, 0.0, dsh).astype(BF16), kr_ref[:, at])
        dq_ref[:, at] = (dq * SCALE).astype(BF16)
        dk_ref[:, at] = (dot_tn(ds, q) * SCALE + from_others(chip_k, core_k, at)).astype(BF16)
        dv_ref[:, at] = (dot_tn(p, ga) + from_others(chip_v, core_v, at)).astype(BF16)


def main_backward(
    ga, att, q, k, v, halo_chip, halo_core, probs, ds_halo, from_chip, from_core, after
):
    rows, feats = q.shape
    groups, col, hk, hv, own, halo = attention_specs(rows, feats)
    return run(
        main_backward_kernel,
        (ga, att, q, k, v, halo_chip, halo_core, probs, ds_halo)
        + (from_chip, from_chip, from_core, from_core),
        [col, col, col, col, col, hk, hk, own, halo, hk, hv, hk, hv],
        [col, col, col],
        [shape((rows, feats))] * 3,
        "main_backward",
        after,
        (groups,),
    )


def first_sends_kernel(k_ref, v_ref, w_ref, c_ref, chip_ref, core_ref, shard_ref, half_ref, held, sems):
    y, core = place()
    rows, feats = k_ref.shape
    parts = 4
    part = feats // parts
    copies = []
    for i, source in enumerate((k_ref, v_ref)):
        for j in range(parts):
            at = pl.ds(j * part, part)
            copies.append((source.at[:, at], held.at[i, :, at]))
    copies.append((w_ref, shard_ref))
    for j in range(parts):
        at = columns((1 - y) * feats + j * part, part)
        copies.append((c_ref.at[:, at], half_ref.at[:, pl.ds(j * part, part)]))
    copies = [pltpu.make_async_copy(*ends, sems.at[i]) for i, ends in enumerate(copies)]
    for copy in copies:
        copy.start()
    for copy in copies:
        copy.wait()
    for i in range(2):
        at = pl.ds(i * feats, feats)
        low, high = held[i, :TILE], held[i, rows - TILE :]
        chip_ref[:, at] = jnp.where(core == 0, low, high)
        core_ref[:, at] = jnp.where(core == 0, high, low)


def first_sends(k, v, w, cot):
    rows, feats = k.shape
    return run(
        first_sends_kernel,
        (k, v, w, cot),
        [pl.BlockSpec(memory_space=pltpu.HBM)] * 4,
        [whole()] * 4,
        [shape((TILE, 2 * feats))] * 2 + [shape(w.shape), shape((rows, cot.shape[1] // 2))],
        "first_sends",
        limit=FIRST,
        scratch_shapes=[pltpu.VMEM((2, rows, feats), BF16), pltpu.SemaphoreType.DMA((13,))],
    )


def core_sends_kernel(cot_ref, partner_ref, att_ref, w_ref, out_ref, att_out, w_out):
    y, core = place()
    rows, width = out_ref.shape[0] // 2, out_ref.shape[1]
    out_ref[:rows] = cot_ref[:, columns((2 * y + 1 - core) * width, width)]
    out_ref[rows:] = partner_ref[:, columns((1 - core) * width, width)]
    att_out[...] = att_ref[...]
    w_out[...] = w_ref[...]


def core_sends(cot, cot_partner, att, shard, after):
    rows, model = cot.shape
    return run(
        core_sends_kernel,
        (cot, cot_partner, att, shard),
        [whole()] * 4,
        [whole()] * 3,
        [shape((2 * rows, model // 4)), shape(att.shape), shape(shard.shape)],
        "core_sends",
        after,
    )


def block_at(shift):
    if not is_grid():
        return shift
    return lax.rem(lax.div(lax.axis_index("dp"), 2) + 4 - shift, 4)


def lay(pair, block):
    x = lax.rem(lax.axis_index("dp"), 2) if is_grid() else 0
    rows = pair[0].shape[0]
    block[rows_at(x * rows, rows), :] = pair[0][...]
    block[rows_at((1 - x) * rows, rows), :] = pair[1][...]


def half_product(c_ref, w_own, w_other, out_ref, sliced):
    y, core = place()
    half = y if sliced else 0
    width = w_own.shape[1]
    total = dot_nt(c_ref[:, columns((2 * half + core) * width, width)], w_own[...])
    total += dot_nt(c_ref[:, columns((2 * half + 1 - core) * width, width)], w_other[...])
    out_ref[...] = total.astype(out_ref.dtype)


def near_kernel(c_ref, w_own, w_other, out_ref, *, sliced):
    half_product(c_ref, w_own, w_other, out_ref, sliced)


def far_kernel(c_ref, own0, own1, other0, other1, out_ref, w_own, w_other, *, sliced):
    lay((own0, own1), w_own)
    lay((other0, other1), w_other)
    half_product(c_ref, w_own, w_other, out_ref, sliced)


def grad_attention_near(cot, near, dtype, sliced, after):
    rows = cot.shape[0]
    return run(
        functools.partial(near_kernel, sliced=sliced),
        (cot, *near),
        [whole()] * 3,
        whole(),
        shape((rows, near[0].shape[0]), dtype),
        "grad_attention_near",
        after,
    )


def grad_attention_far(cot, far, dtype, sliced, after):
    rows = cot.shape[0]
    feats, width = 2 * far[0].shape[0], far[0].shape[1]
    return run(
        functools.partial(far_kernel, sliced=sliced),
        (cot, *far),
        [whole()] * 5,
        whole(),
        shape((rows, feats), dtype),
        "grad_attention_far",
        after,
        scratch_shapes=[pltpu.VMEM((feats, width), BF16)] * 2,
    )


def merge_kernel(own_near, own_far, recv_near, recv_far, out_ref):
    rows, width = own_far.shape
    for i, shift in enumerate((*NEAR, FAR)):
        own, recv = (own_near, recv_near) if i < 3 else (own_far, recv_far)
        at = pl.ds(i * width if i < 3 else 0, width)
        total = own[:, at] + recv[:, at].astype(F32)
        out_ref[:, columns(block_at(shift) * width, width)] = total.astype(BF16)


def merge(own_near, own_far, recv_near, recv_far, after):
    rows, width = own_far.shape
    return run(
        merge_kernel,
        (own_near, own_far, recv_near, recv_far),
        [whole()] * 4,
        whole(),
        shape((rows, 4 * width)),
        "merge",
        after,
    )


def project_kernel(
    a_ref, near_own, near_other, own0, own1, other0, other1, out_ref, far_own, far_other
):
    y, core = place()
    rows, width = far_own.shape
    lay((own0, own1), far_own)
    lay((other0, other1), far_other)
    for quarter, near, far in ((core, near_own, far_own), (1 - core, near_other, far_other)):
        total = dot_nn(a_ref[:, columns(block_at(FAR) * rows, rows)], far[...])
        for i, shift in enumerate(NEAR):
            a = a_ref[:, columns(block_at(shift) * rows, rows)]
            total += dot_nn(a, near[i * rows : (i + 1) * rows])
        out_ref[:, columns(quarter * width, width)] = total.astype(BF16)


def project_half(att, near, far, after):
    rows = att.shape[0]
    feats, width = 2 * far[0].shape[0], far[0].shape[1]
    return run(
        project_kernel,
        (att, *near, *far),
        [whole()] * 7,
        whole(),
        shape((rows, 2 * width)),
        "project_half",
        after,
        scratch_shapes=[pltpu.VMEM((feats, width), BF16)] * 2,
    )


def join_halves_kernel(mine, theirs, out_ref):
    y, core = place()
    width = mine.shape[1]
    out_ref[:, columns(y * width, width)] = mine[...]
    out_ref[:, columns((1 - y) * width, width)] = theirs[...]


def join_halves(mine, theirs):
    rows, width = mine.shape
    return run(
        join_halves_kernel,
        (mine, theirs),
        [whole()] * 2,
        whole(),
        shape((rows, 2 * width)),
        "join_halves",
    )


def assemble_kernel(*refs):
    *pieces, out, sems = refs
    x = lax.rem(lax.axis_index("dp"), 2)
    rows = pieces[0].shape[0]
    copies = []
    for i, piece in enumerate(pieces):
        block = 2 * (i // 2) + (x if i % 2 == 0 else 1 - x)
        copies.append(pltpu.make_async_copy(piece, out.at[rows_at(block * rows, rows)], sems.at[i]))
    for copy in copies:
        copy.start()
    for copy in copies:
        copy.wait()


def assemble(pieces, after):
    rows, width = pieces[0].shape
    n = len(pieces)
    return run(
        assemble_kernel,
        pieces,
        [anywhere()] * n,
        whole(),
        shape((n * rows, width)),
        "assemble_weight",
        after,
        scratch_shapes=[pltpu.SemaphoreType.DMA((n,))],
    )


def along_z(block, shift):
    return lax.ppermute(
        block, "dp", [(2 * z + x, 2 * ((z + shift) % 4) + x) for z in range(4) for x in range(2)]
    )


def across_x(block):
    return lax.ppermute(block, "dp", [(i, i ^ 1) for i in range(8)])


def is_grid():
    return lax.axis_size("dp") == 8


def weight_grad_kernel(
    a_own, a_par, a_sib, a_sibpar, c_own, c_par, c_sib, c_sibpar, *outs_and_total
):
    *outs, total = outs_and_total
    x = lax.rem(lax.axis_index("dp"), 2)
    step = pl.program_id(0)
    half = total.shape[0] // 2
    acc = dot_tn(a_own[...], c_own[...])
    acc += dot_tn(a_par[...], c_par[...])
    acc += dot_tn(a_sib[...], c_sib[...])
    acc += dot_tn(a_sibpar[...], c_sibpar[...])
    total[...] = acc
    keeps, sends = outs[:3], outs[3:]
    for at, (part, row) in enumerate(((0, 0), (1, 0), (1, half), (2, 0))):

        @pl.when(step == at)
        def _():
            keeps[part][row : row + half] = total[rows_at(x * half, half), :]
            sends[part][row : row + half] = total[rows_at((1 - x) * half, half), :].astype(BF16)


def weight_grad_parts(operands, after):
    a_own, a_par, a_sib, a_sibpar, cot, cot_par, c_sib = operands
    tokens, feats = a_own.shape
    width = cot.shape[1] // 4
    part = feats // 4

    def rows_of(g):
        shift = jnp.where(g == 0, 2, jnp.where(g == 1, 1, jnp.where(g == 2, 3, 0)))
        return lax.rem(lax.div(lax.axis_index("dp"), 2) + shift, 4)

    a_spec = pl.BlockSpec((tokens, part), lambda g: (0, rows_of(g)))
    c_specs = [
        pl.BlockSpec((tokens, width), lambda g: (0, lax.axis_index("tile"))),
        pl.BlockSpec((tokens, width), lambda g: (0, lax.rem(lax.axis_index("tile"), 2))),
        pl.BlockSpec((tokens, width), lambda g: (0, 0)),
        pl.BlockSpec((tokens, width), lambda g: (1, 0)),
    ]
    dims = [(part // 2, width), (part, width), (part // 2, width)]
    return run(
        weight_grad_kernel,
        (a_own, a_par, a_sib, a_sibpar, cot, cot_par, c_sib, c_sib),
        [a_spec] * 4 + c_specs,
        [pl.BlockSpec(d, lambda g: (0, 0)) for d in dims * 2],
        [shape(d, F32) for d in dims] + [shape(d) for d in dims],
        "weight_grad_parts",
        after,
        (4,),
        scratch_shapes=[pltpu.VMEM((part, width), F32)],
    )


def weight_grad_sum(operands, after):
    if not is_grid():
        a_own, a_par, a_sib, a_sibpar, cot, cot_par, c_sib = operands
        y, core = place()
        tokens, width = c_sib.shape[0] // 2, c_sib.shape[1]
        c_own = lax.dynamic_slice_in_dim(cot, (2 * y + core) * width, width, axis=1)
        c_par = lax.dynamic_slice_in_dim(cot_par, core * width, width, axis=1)
        total = dot_tn(a_own, c_own) + dot_tn(a_par, c_par)
        total += dot_tn(a_sib, c_sib[:tokens]) + dot_tn(a_sibpar, c_sib[tokens:])
        return lax.psum_scatter(total, "dp", scatter_dimension=0, tiled=True)
    parts = weight_grad_parts(operands, after)
    return (parts[0], across_x(parts[3])), (parts[1], across_x(parts[4])), (parts[2], parts[5])


def add_kernel(*refs):
    *terms, out = refs
    total = terms[0][...].astype(F32)
    for term in terms[1:]:
        total += term[...].astype(F32)
    out[...] = total.astype(out.dtype)


def add(terms, dtype, after=()):
    return run(
        add_kernel,
        terms,
        [whole()] * len(terms),
        whole(),
        shape(terms[0].shape, dtype),
        "add",
        after,
    )


def middle_sums_kernel(keep, recv, from_two, one, three):
    half = one.shape[0]
    one[...] = (keep[:half] + recv[:half].astype(F32) + from_two[...].astype(F32)).astype(BF16)
    three[...] = (keep[half:] + recv[half:].astype(F32)).astype(BF16)


def middle_sums(keep, recv, from_two, after):
    dims = (keep.shape[0] // 2, keep.shape[1])
    return run(
        middle_sums_kernel,
        (keep, recv, from_two),
        [whole()] * 3,
        [whole()] * 2,
        [shape(dims)] * 2,
        "middle_sums",
        after,
    )


def between_chips(block):
    return lax.ppermute(block, "tile", [(1, 2), (2, 1)])


def to_partner(block):
    return lax.ppermute(block, "tile", [(0, 2), (1, 3), (2, 0), (3, 1)])


def to_core(block):
    return lax.ppermute(block, "tile", [(0, 1), (1, 0), (2, 3), (3, 2)])


def shards(queries, key_vectors, value_vectors, out_weight, cotangent):
    q, k, v, cot = queries[0], key_vectors[0], value_vectors[0], cotangent[0]
    tokens = q.shape[0]
    y, core = place()

    rim_chip, rim_core, shard, cot_send = first_sends(k, v, out_weight, cot)
    halo_chip, halo_core = between_chips(rim_chip), to_core(rim_core)
    if is_grid():
        z1, z3 = along_z(shard, 1), along_z(shard, 3)
        x0 = across_x(shard)
    cot_partner = to_partner(cot_send)
    att, probs, probs_halo = attention_forward(q, k, v, halo_chip, halo_core, (z1, z3) if is_grid() else ())
    att_partner = to_partner(att)
    if is_grid():
        x1, x3 = across_x(z1), across_x(z3)
        z2 = relay(along_z(z1, 1), (att,))
        near_own = assemble((shard, x0, z1, x1, z3, x3), (att, cot_partner))
        far_own = (z2, across_x(z2))
    else:
        w_own = lax.all_gather(out_weight, "dp", axis=0, tiled=True)
        cut = w_own.shape[0] * 3 // 4
        near_own = w_own[:cut]
        far_own = (w_own[cut : cut + cut // 6], w_own[cut + cut // 6 :])
    near = (near_own, to_core(near_own))
    cot_send_core, att_send, far_send = core_sends(cot, cot_partner, att, far_own[0], (near_own,))
    cot_core, att_core = to_core(cot_send_core), to_core(att_send)
    far = (*far_own, to_core(far_send), to_core(far_own[1]))

    send_near = grad_attention_near(cot_partner, near, BF16, False, (cot_send_core,))
    recv_near = to_partner(send_near)
    send_far = grad_attention_far(cot_partner, far, BF16, False, (send_near,))
    recv_far = to_partner(send_far)

    att_partner = relay(att_partner, (send_far,))
    att_core_partner = to_core(att_partner)
    mine_near = grad_attention_near(cot, near, F32, True, (send_far,))
    parts = weight_grad_sum(
        (att, att_partner, att_core, att_core_partner, cot, cot_partner, cot_core), (mine_near,)
    )
    grid = is_grid()
    mine_far = grad_attention_far(
        cot, far, F32, True, (mine_near, parts[2][0]) if grid else (mine_near,)
    )
    proj_partner = project_half(att_partner, near, far, (mine_far,))
    proj_recv = to_partner(proj_partner)
    if grid:
        far_sum = add(parts[0], BF16, (proj_partner,))
        from_two = along_z(far_sum, 1)
        recv = across_x(relay(parts[2][1], (far_sum,)))

    ga = merge(mine_near, mine_far, recv_near, recv_far, (far_sum,) if grid else ())
    ds_halo, back_chip, back_core = halo_backward(ga, att, q, halo_chip, halo_core, probs_halo)
    from_chip, from_core = between_chips(back_chip), to_core(back_core)
    if grid:
        one, three = middle_sums(*parts[1], from_two, (ds_halo,))
        from_one, from_three = along_z(one, 1), along_z(three, 3)
    proj_own = project_half(att, near, far, (one,) if grid else (proj_partner,))
    dq, dk, dv = main_backward(
        ga, att, q, k, v, halo_chip, halo_core, probs, ds_halo, from_chip, from_core, (proj_own,)
    )
    projected = join_halves(proj_own, proj_recv)
    weight_grad = add((parts[2][0], recv, from_three, from_one), F32, (dq,)) if grid else parts
    return projected[None], dq[None], dk[None], dv[None], weight_grad


def solution(mesh):
    tokens = P("dp", "tile", None)
    weight = P("dp", "tile")
    return jax.shard_map(
        shards,
        mesh=mesh,
        in_specs=(tokens, tokens, tokens, weight, tokens),
        out_specs=(tokens, tokens, tokens, tokens, weight),
        check_vma=False,
    )
```

```python
import functools

import jax
import jax.numpy as jnp
from jax import lax
from jax.experimental import pallas as pl
from jax.experimental.pallas import tpu as pltpu
from jax.sharding import PartitionSpec as P

HEADS = 12
HEAD = 128
TILE = 120
GROUP = 3
NEAR = (0, 1, 3)
FAR = 2
SCALE = HEAD**-0.5
VMEM = 32 * 1024 * 1024
FIRST = 60 * 1024 * 1024
BF16 = jnp.bfloat16
F32 = jnp.float32


def dot_nn(a, b):
    return lax.dot_general(a, b, (((1,), (0,)), ((), ())), preferred_element_type=F32)


def dot_nt(a, b):
    return lax.dot_general(a, b, (((1,), (1,)), ((), ())), preferred_element_type=F32)


def dot_tn(a, b):
    return lax.dot_general(a, b, (((0,), (0,)), ((), ())), preferred_element_type=F32)


WEIGHT = {}


def cost(name):
    return pl.CostEstimate(
        flops=int(WEIGHT.get(name, 3e10)), bytes_accessed=int(1e10), transcendentals=0
    )


def whole():
    return pl.BlockSpec(memory_space=pltpu.VMEM)


def anywhere():
    return pl.BlockSpec(memory_space=pl.ANY)


def shape(dims, dtype=BF16):
    return jax.ShapeDtypeStruct(dims, dtype)


def run(kernel, args, in_specs, out_specs, out_shape, name, after=(), grid=(), limit=VMEM, **extra):
    count, skipped = len(args), len(after)

    def body(*refs):
        kernel(*refs[:count], *refs[count + skipped :])

    return pl.pallas_call(
        body,
        grid=grid,
        in_specs=list(in_specs) + [anywhere()] * skipped,
        out_specs=out_specs,
        out_shape=out_shape,
        compiler_params=pltpu.CompilerParams(vmem_limit_bytes=limit),
        cost_estimate=cost(name),
        name=name,
        **extra,
    )(*args, *after)


def relay(block, after):
    def body(*refs):
        pass

    return pl.pallas_call(
        body,
        in_specs=[anywhere()] * (1 + len(after)),
        out_specs=anywhere(),
        out_shape=shape(block.shape, block.dtype),
        input_output_aliases={0: 0},
        cost_estimate=cost("relay"),
        name="relay",
    )(block, *after)


def facing_rows(rows, cols):
    y, core = place()
    top = lax.broadcasted_iota(jnp.int32, (rows, cols), 0) < TILE
    return top == (core == 0)


def place():
    tile = lax.axis_index("tile")
    return lax.div(tile, 2), lax.rem(tile, 2)


def columns(start, width):
    return pl.ds(pl.multiple_of(start, 128), width)


def rows_at(start, count):
    return pl.ds(pl.multiple_of(start, 16), count)


def forward_kernel(q_ref, k_ref, v_ref, kl_ref, vl_ref, kr_ref, vr_ref, a_ref, p_ref, ph_ref):
    rows = q_ref.shape[0]
    y, core = place()
    facing = facing_rows(rows, TILE)
    seen = jnp.logical_not(facing) | (y != core)
    for h in range(GROUP):
        at = pl.ds(h * HEAD, HEAD)
        q = q_ref[:, at]
        s = dot_nt(q, k_ref[:, at]) * SCALE
        sh = jnp.where(facing, dot_nt(q, kl_ref[:, at]), dot_nt(q, kr_ref[:, at])) * SCALE
        sh = jnp.where(seen, sh, -1e30)
        top_score = jnp.maximum(
            jnp.max(s, axis=-1, keepdims=True), jnp.max(sh, axis=-1, keepdims=True)
        )
        e = jnp.exp(s - top_score)
        eh = jnp.exp(sh - top_score)
        total = jnp.sum(e, axis=-1, keepdims=True) + jnp.sum(eh, axis=-1, keepdims=True)
        inverse = 1.0 / total
        p = (e * inverse).astype(BF16)
        ph = eh * inverse
        p_ref[h] = p
        ph_ref[h] = ph.astype(BF16)
        out = dot_nn(p, v_ref[:, at])
        out += dot_nn(jnp.where(facing, ph, 0.0).astype(BF16), vl_ref[:, at])
        out += dot_nn(jnp.where(facing, 0.0, ph).astype(BF16), vr_ref[:, at])
        a_ref[:, at] = out.astype(BF16)


def attention_specs(rows, feats):
    width = GROUP * HEAD
    groups = feats // width
    col = pl.BlockSpec((rows, width), lambda g: (0, g))
    halo_keys = pl.BlockSpec((TILE, width), lambda g: (0, g))
    halo_values = pl.BlockSpec((TILE, width), lambda g: (0, groups + g))
    own = pl.BlockSpec((GROUP, rows, rows), lambda g: (g, 0, 0))
    halo = pl.BlockSpec((GROUP, rows, TILE), lambda g: (g, 0, 0))
    return groups, col, halo_keys, halo_values, own, halo


def attention_forward(q, k, v, halo_chip, halo_core, after):
    rows, feats = q.shape
    groups, col, hk, hv, own, halo = attention_specs(rows, feats)
    return run(
        forward_kernel,
        (q, k, v, halo_chip, halo_chip, halo_core, halo_core),
        [col, col, col, hk, hv, hk, hv],
        [col, own, halo],
        [
            shape((rows, feats)),
            pltpu.HBM((HEADS, rows, rows), BF16),
            pltpu.HBM((HEADS, rows, TILE), BF16),
        ],
        "attention_forward",
        after,
        (groups,),
    )


def halo_backward_kernel(
    ga_ref, a_ref, q_ref, vl_ref, vr_ref, ph_ref, ds_ref, chip_ref, core_ref
):
    rows = q_ref.shape[0]
    feats = chip_ref.shape[1] // 2
    facing = facing_rows(rows, TILE)
    first = pl.program_id(0) * (GROUP * HEAD)
    for h in range(GROUP):
        at = pl.ds(h * HEAD, HEAD)
        to_key = columns(first + h * HEAD, HEAD)
        to_value = columns(first + feats + h * HEAD, HEAD)
        q = q_ref[:, at]
        ga = ga_ref[:, at]
        dots = jnp.sum(ga.astype(F32) * a_ref[:, at].astype(F32), axis=-1, keepdims=True)
        dp = jnp.where(facing, dot_nt(ga, vl_ref[:, at]), dot_nt(ga, vr_ref[:, at]))
        ph = ph_ref[h].astype(F32)
        ds = ph * (dp - dots)
        ds_ref[h] = ds.astype(BF16)
        chip_ref[:, to_key] = (dot_tn(jnp.where(facing, ds, 0.0).astype(BF16), q) * SCALE).astype(BF16)
        core_ref[:, to_key] = (dot_tn(jnp.where(facing, 0.0, ds).astype(BF16), q) * SCALE).astype(BF16)
        chip_ref[:, to_value] = dot_tn(jnp.where(facing, ph, 0.0).astype(BF16), ga).astype(BF16)
        core_ref[:, to_value] = dot_tn(jnp.where(facing, 0.0, ph).astype(BF16), ga).astype(BF16)


def halo_backward(ga, att, q, halo_chip, halo_core, probs_halo):
    rows, feats = q.shape
    groups, col, hk, hv, own, halo = attention_specs(rows, feats)
    rim = pl.BlockSpec((TILE, 2 * feats), lambda g: (0, 0))
    return run(
        halo_backward_kernel,
        (ga, att, q, halo_chip, halo_core, probs_halo),
        [col, col, col, hv, hv, halo],
        [halo, rim, rim],
        [shape((HEADS, rows, TILE))] + [shape((TILE, 2 * feats))] * 2,
        "halo_backward",
        (),
        (groups,),
    )


def main_backward_kernel(
    ga_ref,
    a_ref,
    q_ref,
    k_ref,
    v_ref,
    kl_ref,
    kr_ref,
    p_ref,
    dsh_ref,
    chip_k,
    chip_v,
    core_k,
    core_v,
    dq_ref,
    dk_ref,
    dv_ref,
):
    rows = q_ref.shape[0]
    y, core = place()
    facing = facing_rows(rows, TILE)

    def from_others(chip, other, at):
        far, near = chip[:, at].astype(F32), other[:, at].astype(F32)
        low, high = jnp.where(core == 0, far, near), jnp.where(core == 0, near, far)
        return jnp.concatenate([low, high], axis=0)

    for h in range(GROUP):
        at = pl.ds(h * HEAD, HEAD)
        q = q_ref[:, at]
        ga = ga_ref[:, at]
        dots = jnp.sum(ga.astype(F32) * a_ref[:, at].astype(F32), axis=-1, keepdims=True)
        p = p_ref[h]
        ds = (p.astype(F32) * (dot_nt(ga, v_ref[:, at]) - dots)).astype(BF16)
        dsh = dsh_ref[h].astype(F32)
        dq = dot_nn(ds, k_ref[:, at])
        dq += dot_nn(jnp.where(facing, dsh, 0.0).astype(BF16), kl_ref[:, at])
        dq += dot_nn(jnp.where(facing, 0.0, dsh).astype(BF16), kr_ref[:, at])
        dq_ref[:, at] = (dq * SCALE).astype(BF16)
        dk_ref[:, at] = (dot_tn(ds, q) * SCALE + from_others(chip_k, core_k, at)).astype(BF16)
        dv_ref[:, at] = (dot_tn(p, ga) + from_others(chip_v, core_v, at)).astype(BF16)


def main_backward(
    ga, att, q, k, v, halo_chip, halo_core, probs, ds_halo, from_chip, from_core, after
):
    rows, feats = q.shape
    groups, col, hk, hv, own, halo = attention_specs(rows, feats)
    return run(
        main_backward_kernel,
        (ga, att, q, k, v, halo_chip, halo_core, probs, ds_halo)
        + (from_chip, from_chip, from_core, from_core),
        [col, col, col, col, col, hk, hk, own, halo, hk, hv, hk, hv],
        [col, col, col],
        [shape((rows, feats))] * 3,
        "main_backward",
        after,
        (groups,),
    )


def first_sends_kernel(k_ref, v_ref, w_ref, c_ref, chip_ref, core_ref, shard_ref, half_ref, held, sems):
    y, core = place()
    rows, feats = k_ref.shape
    parts = 4
    part = feats // parts
    copies = []
    for i, source in enumerate((k_ref, v_ref)):
        for j in range(parts):
            at = pl.ds(j * part, part)
            copies.append((source.at[:, at], held.at[i, :, at]))
    copies.append((w_ref, shard_ref))
    for j in range(parts):
        at = columns((1 - y) * feats + j * part, part)
        copies.append((c_ref.at[:, at], half_ref.at[:, pl.ds(j * part, part)]))
    copies = [pltpu.make_async_copy(*ends, sems.at[i]) for i, ends in enumerate(copies)]
    for copy in copies:
        copy.start()
    for copy in copies:
        copy.wait()
    for i in range(2):
        at = pl.ds(i * feats, feats)
        low, high = held[i, :TILE], held[i, rows - TILE :]
        chip_ref[:, at] = jnp.where(core == 0, low, high)
        core_ref[:, at] = jnp.where(core == 0, high, low)


def first_sends(k, v, w, cot):
    rows, feats = k.shape
    return run(
        first_sends_kernel,
        (k, v, w, cot),
        [pl.BlockSpec(memory_space=pltpu.HBM)] * 4,
        [whole()] * 4,
        [shape((TILE, 2 * feats))] * 2 + [shape(w.shape), shape((rows, cot.shape[1] // 2))],
        "first_sends",
        limit=FIRST,
        scratch_shapes=[pltpu.VMEM((2, rows, feats), BF16), pltpu.SemaphoreType.DMA((13,))],
    )


def core_sends_kernel(cot_ref, partner_ref, att_ref, w_ref, out_ref, att_out, w_out):
    y, core = place()
    rows, width = out_ref.shape[0] // 2, out_ref.shape[1]
    out_ref[:rows] = cot_ref[:, columns((2 * y + 1 - core) * width, width)]
    out_ref[rows:] = partner_ref[:, columns((1 - core) * width, width)]
    att_out[...] = att_ref[...]
    w_out[...] = w_ref[...]


def core_sends(cot, cot_partner, att, shard, after):
    rows, model = cot.shape
    return run(
        core_sends_kernel,
        (cot, cot_partner, att, shard),
        [whole()] * 4,
        [whole()] * 3,
        [shape((2 * rows, model // 4)), shape(att.shape), shape(shard.shape)],
        "core_sends",
        after,
    )


def block_at(shift):
    if not is_grid():
        return shift
    return lax.rem(lax.div(lax.axis_index("dp"), 2) + 4 - shift, 4)


def lay(pair, block):
    x = lax.rem(lax.axis_index("dp"), 2) if is_grid() else 0
    rows = pair[0].shape[0]
    block[rows_at(x * rows, rows), :] = pair[0][...]
    block[rows_at((1 - x) * rows, rows), :] = pair[1][...]


def half_product(c_ref, w_own, w_other, out_ref, sliced):
    y, core = place()
    half = y if sliced else 0
    width = w_own.shape[1]
    total = dot_nt(c_ref[:, columns((2 * half + core) * width, width)], w_own[...])
    total += dot_nt(c_ref[:, columns((2 * half + 1 - core) * width, width)], w_other[...])
    out_ref[...] = total.astype(out_ref.dtype)


def near_kernel(c_ref, w_own, w_other, out_ref, *, sliced):
    half_product(c_ref, w_own, w_other, out_ref, sliced)


def far_kernel(c_ref, own0, own1, other0, other1, out_ref, w_own, w_other, *, sliced):
    lay((own0, own1), w_own)
    lay((other0, other1), w_other)
    half_product(c_ref, w_own, w_other, out_ref, sliced)


def grad_attention_near(cot, near, dtype, sliced, after):
    rows = cot.shape[0]
    return run(
        functools.partial(near_kernel, sliced=sliced),
        (cot, *near),
        [whole()] * 3,
        whole(),
        shape((rows, near[0].shape[0]), dtype),
        "grad_attention_near",
        after,
    )


def grad_attention_far(cot, far, dtype, sliced, after):
    rows = cot.shape[0]
    feats, width = 2 * far[0].shape[0], far[0].shape[1]
    return run(
        functools.partial(far_kernel, sliced=sliced),
        (cot, *far),
        [whole()] * 5,
        whole(),
        shape((rows, feats), dtype),
        "grad_attention_far",
        after,
        scratch_shapes=[pltpu.VMEM((feats, width), BF16)] * 2,
    )


def merge_kernel(own_near, own_far, recv_near, recv_far, out_ref):
    rows, width = own_far.shape
    for i, shift in enumerate((*NEAR, FAR)):
        own, recv = (own_near, recv_near) if i < 3 else (own_far, recv_far)
        at = pl.ds(i * width if i < 3 else 0, width)
        total = own[:, at].astype(F32) + recv[:, at].astype(F32)
        out_ref[:, columns(block_at(shift) * width, width)] = total.astype(BF16)


def merge(own_near, own_far, recv_near, recv_far, after):
    rows, width = own_far.shape
    return run(
        merge_kernel,
        (own_near, own_far, recv_near, recv_far),
        [whole()] * 4,
        whole(),
        shape((rows, 4 * width)),
        "merge",
        after,
    )


def project_kernel(
    a_own, a_par, near_own, near_other, own0, own1, other0, other1, mine, theirs, far_own, far_other
):
    y, core = place()
    rows, width = far_own.shape
    lay((own0, own1), far_own)
    lay((other0, other1), far_other)
    for quarter, near, far in ((core, near_own, far_own), (1 - core, near_other, far_other)):
        for a_ref, out_ref in ((a_par, theirs), (a_own, mine)):
            total = dot_nn(a_ref[:, columns(block_at(FAR) * rows, rows)], far[...])
            for i, shift in enumerate(NEAR):
                a = a_ref[:, columns(block_at(shift) * rows, rows)]
                total += dot_nn(a, near[i * rows : (i + 1) * rows])
            out_ref[:, columns(quarter * width, width)] = total.astype(BF16)


def project_half(att, att_partner, near, far, after):
    rows, feats = att.shape
    feats, width = 2 * far[0].shape[0], far[0].shape[1]
    return run(
        project_kernel,
        (att, att_partner, *near, *far),
        [whole()] * 8,
        [whole()] * 2,
        [shape((rows, 2 * width))] * 2,
        "project_half",
        after,
        scratch_shapes=[pltpu.VMEM((feats, width), BF16)] * 2,
    )


def join_halves_kernel(mine, theirs, out_ref):
    y, core = place()
    width = mine.shape[1]
    out_ref[:, columns(y * width, width)] = mine[...]
    out_ref[:, columns((1 - y) * width, width)] = theirs[...]


def join_halves(mine, theirs):
    rows, width = mine.shape
    return run(
        join_halves_kernel,
        (mine, theirs),
        [whole()] * 2,
        whole(),
        shape((rows, 2 * width)),
        "join_halves",
    )


def assemble_kernel(*refs):
    *pieces, out, sems = refs
    x = lax.rem(lax.axis_index("dp"), 2)
    rows = pieces[0].shape[0]
    copies = []
    for i, piece in enumerate(pieces):
        block = 2 * (i // 2) + (x if i % 2 == 0 else 1 - x)
        copies.append(pltpu.make_async_copy(piece, out.at[rows_at(block * rows, rows)], sems.at[i]))
    for copy in copies:
        copy.start()
    for copy in copies:
        copy.wait()


def assemble(pieces, after):
    rows, width = pieces[0].shape
    n = len(pieces)
    return run(
        assemble_kernel,
        pieces,
        [anywhere()] * n,
        whole(),
        shape((n * rows, width)),
        "assemble_weight",
        after,
        scratch_shapes=[pltpu.SemaphoreType.DMA((n,))],
    )


def along_z(block, shift):
    return lax.ppermute(
        block, "dp", [(2 * z + x, 2 * ((z + shift) % 4) + x) for z in range(4) for x in range(2)]
    )


def across_x(block):
    return lax.ppermute(block, "dp", [(i, i ^ 1) for i in range(8)])


def is_grid():
    return lax.axis_size("dp") == 8


def weight_grad_kernel(
    a_own, a_par, a_sib, a_sibpar, c_own, c_par, c_sib, c_sibpar, *outs_and_total
):
    *outs, total = outs_and_total
    x = lax.rem(lax.axis_index("dp"), 2)
    step = pl.program_id(0)
    half = total.shape[0] // 2
    acc = dot_tn(a_own[...], c_own[...])
    acc += dot_tn(a_par[...], c_par[...])
    acc += dot_tn(a_sib[...], c_sib[...])
    acc += dot_tn(a_sibpar[...], c_sibpar[...])
    total[...] = acc
    keep, *sends = outs
    keep[...] = total[rows_at(x * half, half), :].astype(BF16)
    for at, (part, row) in enumerate(((0, 0), (1, 0), (1, half), (2, 0))):

        @pl.when(step == at)
        def _():
            sends[part][row : row + half] = total[rows_at((1 - x) * half, half), :].astype(BF16)


def weight_grad_parts(operands, after):
    a_own, a_par, a_sib, a_sibpar, cot, cot_par, c_sib = operands
    tokens, feats = a_own.shape
    width = cot.shape[1] // 4
    part = feats // 4

    def rows_of(g):
        shift = jnp.where(g == 0, 2, jnp.where(g == 1, 1, jnp.where(g == 2, 3, 0)))
        return lax.rem(lax.div(lax.axis_index("dp"), 2) + shift, 4)

    a_spec = pl.BlockSpec((tokens, part), lambda g: (0, rows_of(g)))
    c_specs = [
        pl.BlockSpec((tokens, width), lambda g: (0, lax.axis_index("tile"))),
        pl.BlockSpec((tokens, width), lambda g: (0, lax.rem(lax.axis_index("tile"), 2))),
        pl.BlockSpec((tokens, width), lambda g: (0, 0)),
        pl.BlockSpec((tokens, width), lambda g: (1, 0)),
    ]
    dims = [(part // 2, width), (part, width), (part // 2, width)]
    return run(
        weight_grad_kernel,
        (a_own, a_par, a_sib, a_sibpar, cot, cot_par, c_sib, c_sib),
        [a_spec] * 4 + c_specs,
        [pl.BlockSpec((part // 2, width), lambda g: (g, 0))]
        + [pl.BlockSpec(d, lambda g: (0, 0)) for d in dims],
        [shape((2 * part, width))] + [shape(d) for d in dims],
        "weight_grad_parts",
        after,
        (4,),
        scratch_shapes=[pltpu.VMEM((part, width), F32)],
    )


def weight_grad_sum(operands, after):
    if not is_grid():
        a_own, a_par, a_sib, a_sibpar, cot, cot_par, c_sib = operands
        y, core = place()
        tokens, width = c_sib.shape[0] // 2, c_sib.shape[1]
        c_own = lax.dynamic_slice_in_dim(cot, (2 * y + core) * width, width, axis=1)
        c_par = lax.dynamic_slice_in_dim(cot_par, core * width, width, axis=1)
        total = dot_tn(a_own, c_own) + dot_tn(a_par, c_par)
        total += dot_tn(a_sib, c_sib[:tokens]) + dot_tn(a_sibpar, c_sib[tokens:])
        return lax.psum_scatter(total, "dp", scatter_dimension=0, tiled=True)
    parts = weight_grad_parts(operands, after)
    return parts[0], across_x(parts[1]), across_x(parts[2]), parts[3]


def kept(keep, slot):
    rows, width = keep.shape
    return pl.BlockSpec((rows // 4, width), lambda g: (slot, 0))


def one_step(block):
    return pl.BlockSpec(block.shape, lambda g: (0, 0))


def add_kernel(*refs):
    *terms, out = refs
    total = terms[0][...].astype(F32)
    for term in terms[1:]:
        total += term[...].astype(F32)
    out[...] = total.astype(out.dtype)


def add(first, spec, terms, dtype, after=()):
    return run(
        add_kernel,
        (first, *terms),
        [spec] + [one_step(term) for term in terms],
        one_step(terms[0]),
        shape(terms[0].shape, dtype),
        "add",
        after,
        (1,),
    )


def middle_sums_kernel(keep_one, keep_three, recv, from_two, one, three):
    half = one.shape[0]
    total = keep_one[...].astype(F32) + recv[:half].astype(F32) + from_two[...].astype(F32)
    one[...] = total.astype(BF16)
    three[...] = (keep_three[...].astype(F32) + recv[half:].astype(F32)).astype(BF16)


def middle_sums(keep, recv, from_two, after):
    return run(
        middle_sums_kernel,
        (keep, keep, recv, from_two),
        [kept(keep, 1), kept(keep, 2), one_step(recv), one_step(from_two)],
        [one_step(from_two)] * 2,
        [shape(from_two.shape)] * 2,
        "middle_sums",
        after,
        (1,),
    )


def between_chips(block):
    return lax.ppermute(block, "tile", [(1, 2), (2, 1)])


def to_partner(block):
    return lax.ppermute(block, "tile", [(0, 2), (1, 3), (2, 0), (3, 1)])


def to_core(block):
    return lax.ppermute(block, "tile", [(0, 1), (1, 0), (2, 3), (3, 2)])


def shards(queries, key_vectors, value_vectors, out_weight, cotangent):
    q, k, v, cot = queries[0], key_vectors[0], value_vectors[0], cotangent[0]
    tokens = q.shape[0]
    y, core = place()

    rim_chip, rim_core, shard, cot_send = first_sends(k, v, out_weight, cot)
    halo_chip, halo_core = between_chips(rim_chip), to_core(rim_core)
    if is_grid():
        z1, z3 = along_z(shard, 1), along_z(shard, 3)
        x0 = across_x(shard)
    cot_partner = to_partner(cot_send)
    att, probs, probs_halo = attention_forward(q, k, v, halo_chip, halo_core, (z1, z3) if is_grid() else ())
    att_partner = to_partner(att)
    if is_grid():
        x1, x3 = across_x(z1), across_x(z3)
        z2 = relay(along_z(z1, 1), (att,))
        near_own = assemble((shard, x0, z1, x1, z3, x3), (att, cot_partner))
        far_own = (z2, across_x(z2))
    else:
        w_own = lax.all_gather(out_weight, "dp", axis=0, tiled=True)
        cut = w_own.shape[0] * 3 // 4
        near_own = w_own[:cut]
        far_own = (w_own[cut : cut + cut // 6], w_own[cut + cut // 6 :])
    near = (near_own, to_core(near_own))
    cot_send_core, att_send, far_send = core_sends(cot, cot_partner, att, far_own[0], (near_own,))
    cot_core, att_core = to_core(cot_send_core), to_core(att_send)
    far = (*far_own, to_core(far_send), to_core(far_own[1]))

    send_near = grad_attention_near(cot_partner, near, BF16, False, (cot_send_core,))
    recv_near = to_partner(send_near)
    send_far = grad_attention_far(cot_partner, far, BF16, False, (send_near,))
    recv_far = to_partner(send_far)

    att_partner = relay(att_partner, (send_far,))
    att_core_partner = to_core(att_partner)
    mine_near = grad_attention_near(cot, near, BF16, True, (send_far,))
    parts = weight_grad_sum(
        (att, att_partner, att_core, att_core_partner, cot, cot_partner, cot_core), (mine_near,)
    )
    grid = is_grid()
    mine_far = grad_attention_far(
        cot, far, BF16, True, (mine_near, parts[0]) if grid else (mine_near,)
    )
    proj_own, proj_partner = project_half(att, att_partner, near, far, (mine_far,))
    proj_recv = to_partner(proj_partner)
    if grid:
        far_sum = add(parts[0], kept(parts[0], 0), (parts[1],), BF16, (proj_partner,))
        from_two = along_z(far_sum, 1)
        recv = across_x(relay(parts[3], (far_sum,)))

    ga = merge(mine_near, mine_far, recv_near, recv_far, (far_sum,) if grid else ())
    ds_halo, back_chip, back_core = halo_backward(ga, att, q, halo_chip, halo_core, probs_halo)
    from_chip, from_core = between_chips(back_chip), to_core(back_core)
    if grid:
        one, three = middle_sums(parts[0], parts[2], from_two, (ds_halo,))
        from_one, from_three = along_z(one, 1), along_z(three, 3)
    dq, dk, dv = main_backward(
        ga, att, q, k, v, halo_chip, halo_core, probs, ds_halo, from_chip, from_core, (one,) if grid else ()
    )
    projected = join_halves(proj_own, proj_recv)
    weight_grad = parts
    if grid:
        near_sum = add(parts[0], kept(parts[0], 3), (recv, from_three), F32, (dq,))
        weight_grad = add(near_sum, one_step(near_sum), (from_one,), F32)
    return projected[None], dq[None], dk[None], dv[None], weight_grad


def solution(mesh):
    tokens = P("dp", "tile", None)
    weight = P("dp", "tile")
    return jax.shard_map(
        shards,
        mesh=mesh,
        in_specs=(tokens, tokens, tokens, weight, tokens),
        out_specs=(tokens, tokens, tokens, tokens, weight),
        check_vma=False,
    )
```

```python
import functools

import jax
import jax.numpy as jnp
from jax import lax
from jax.experimental import pallas as pl
from jax.experimental.pallas import tpu as pltpu
from jax.sharding import PartitionSpec as P

HEADS = 12
HEAD = 128
TILE = 120
GROUP = 3
NEAR = (0, 1, 3)
FAR = 2
SCALE = HEAD**-0.5
VMEM = 32 * 1024 * 1024
FIRST = 60 * 1024 * 1024
BF16 = jnp.bfloat16
F32 = jnp.float32


def dot_nn(a, b):
    return lax.dot_general(a, b, (((1,), (0,)), ((), ())), preferred_element_type=F32)


def dot_nt(a, b):
    return lax.dot_general(a, b, (((1,), (1,)), ((), ())), preferred_element_type=F32)


def dot_tn(a, b):
    return lax.dot_general(a, b, (((0,), (0,)), ((), ())), preferred_element_type=F32)


WEIGHT = {}


def cost(name):
    return pl.CostEstimate(
        flops=int(WEIGHT.get(name, 3e10)), bytes_accessed=int(1e10), transcendentals=0
    )


def whole():
    return pl.BlockSpec(memory_space=pltpu.VMEM)


def anywhere():
    return pl.BlockSpec(memory_space=pl.ANY)


def shape(dims, dtype=BF16):
    return jax.ShapeDtypeStruct(dims, dtype)


def run(kernel, args, in_specs, out_specs, out_shape, name, after=(), grid=(), limit=VMEM, **extra):
    count, skipped = len(args), len(after)

    def body(*refs):
        kernel(*refs[:count], *refs[count + skipped :])

    return pl.pallas_call(
        body,
        grid=grid,
        in_specs=list(in_specs) + [anywhere()] * skipped,
        out_specs=out_specs,
        out_shape=out_shape,
        compiler_params=pltpu.CompilerParams(vmem_limit_bytes=limit),
        cost_estimate=cost(name),
        name=name,
        **extra,
    )(*args, *after)


def relay(block, after):
    def body(*refs):
        pass

    return pl.pallas_call(
        body,
        in_specs=[anywhere()] * (1 + len(after)),
        out_specs=anywhere(),
        out_shape=shape(block.shape, block.dtype),
        input_output_aliases={0: 0},
        cost_estimate=cost("relay"),
        name="relay",
    )(block, *after)


def facing_rows(rows, cols):
    y, core = place()
    top = lax.broadcasted_iota(jnp.int32, (rows, cols), 0) < TILE
    return top == (core == 0)


def place():
    tile = lax.axis_index("tile")
    return lax.div(tile, 2), lax.rem(tile, 2)


def columns(start, width):
    return pl.ds(pl.multiple_of(start, 128), width)


def rows_at(start, count):
    return pl.ds(pl.multiple_of(start, 16), count)


def forward_kernel(q_ref, k_ref, v_ref, kl_ref, vl_ref, kr_ref, vr_ref, a_ref, p_ref, ph_ref):
    rows = q_ref.shape[0]
    y, core = place()
    facing = facing_rows(rows, TILE)
    seen = jnp.logical_not(facing) | (y != core)
    for h in range(GROUP):
        at = pl.ds(h * HEAD, HEAD)
        q = q_ref[:, at]
        s = dot_nt(q, k_ref[:, at]) * SCALE
        sh = jnp.where(facing, dot_nt(q, kl_ref[:, at]), dot_nt(q, kr_ref[:, at])) * SCALE
        sh = jnp.where(seen, sh, -1e30)
        top_score = jnp.maximum(
            jnp.max(s, axis=-1, keepdims=True), jnp.max(sh, axis=-1, keepdims=True)
        )
        e = jnp.exp(s - top_score)
        eh = jnp.exp(sh - top_score)
        total = jnp.sum(e, axis=-1, keepdims=True) + jnp.sum(eh, axis=-1, keepdims=True)
        inverse = 1.0 / total
        p = (e * inverse).astype(BF16)
        ph = eh * inverse
        p_ref[h] = p
        ph_ref[h] = ph.astype(BF16)
        out = dot_nn(p, v_ref[:, at])
        out += dot_nn(jnp.where(facing, ph, 0.0).astype(BF16), vl_ref[:, at])
        out += dot_nn(jnp.where(facing, 0.0, ph).astype(BF16), vr_ref[:, at])
        a_ref[:, at] = out.astype(BF16)


def attention_specs(rows, feats):
    width = GROUP * HEAD
    groups = feats // width
    col = pl.BlockSpec((rows, width), lambda g: (0, g))
    halo_keys = pl.BlockSpec((TILE, width), lambda g: (0, g))
    halo_values = pl.BlockSpec((TILE, width), lambda g: (0, groups + g))
    own = pl.BlockSpec((GROUP, rows, rows), lambda g: (g, 0, 0))
    halo = pl.BlockSpec((GROUP, rows, TILE), lambda g: (g, 0, 0))
    return groups, col, halo_keys, halo_values, own, halo


def attention_forward(q, k, v, halo_chip, halo_core, after):
    rows, feats = q.shape
    groups, col, hk, hv, own, halo = attention_specs(rows, feats)
    return run(
        forward_kernel,
        (q, k, v, halo_chip, halo_chip, halo_core, halo_core),
        [col, col, col, hk, hv, hk, hv],
        [col, own, halo],
        [
            shape((rows, feats)),
            pltpu.HBM((HEADS, rows, rows), BF16),
            pltpu.HBM((HEADS, rows, TILE), BF16),
        ],
        "attention_forward",
        after,
        (groups,),
    )


def halo_backward_kernel(
    ga_ref, a_ref, q_ref, vl_ref, vr_ref, ph_ref, ds_ref, chip_ref, core_ref
):
    rows = q_ref.shape[0]
    feats = chip_ref.shape[1] // 2
    facing = facing_rows(rows, TILE)
    first = pl.program_id(0) * (GROUP * HEAD)
    for h in range(GROUP):
        at = pl.ds(h * HEAD, HEAD)
        to_key = columns(first + h * HEAD, HEAD)
        to_value = columns(first + feats + h * HEAD, HEAD)
        q = q_ref[:, at]
        ga = ga_ref[:, at]
        dots = jnp.sum(ga.astype(F32) * a_ref[:, at].astype(F32), axis=-1, keepdims=True)
        dp = jnp.where(facing, dot_nt(ga, vl_ref[:, at]), dot_nt(ga, vr_ref[:, at]))
        ph = ph_ref[h].astype(F32)
        ds = ph * (dp - dots)
        ds_ref[h] = ds.astype(BF16)
        chip_ref[:, to_key] = (dot_tn(jnp.where(facing, ds, 0.0).astype(BF16), q) * SCALE).astype(BF16)
        core_ref[:, to_key] = (dot_tn(jnp.where(facing, 0.0, ds).astype(BF16), q) * SCALE).astype(BF16)
        chip_ref[:, to_value] = dot_tn(jnp.where(facing, ph, 0.0).astype(BF16), ga).astype(BF16)
        core_ref[:, to_value] = dot_tn(jnp.where(facing, 0.0, ph).astype(BF16), ga).astype(BF16)


def halo_backward(ga, att, q, halo_chip, halo_core, probs_halo):
    rows, feats = q.shape
    groups, col, hk, hv, own, halo = attention_specs(rows, feats)
    rim = pl.BlockSpec((TILE, 2 * feats), lambda g: (0, 0))
    return run(
        halo_backward_kernel,
        (ga, att, q, halo_chip, halo_core, probs_halo),
        [col, col, col, hv, hv, halo],
        [halo, rim, rim],
        [shape((HEADS, rows, TILE))] + [shape((TILE, 2 * feats))] * 2,
        "halo_backward",
        (),
        (groups,),
    )


def main_backward_kernel(
    ga_ref,
    a_ref,
    q_ref,
    k_ref,
    v_ref,
    kl_ref,
    kr_ref,
    p_ref,
    dsh_ref,
    chip_k,
    chip_v,
    core_k,
    core_v,
    dq_ref,
    dk_ref,
    dv_ref,
):
    rows = q_ref.shape[0]
    y, core = place()
    facing = facing_rows(rows, TILE)

    def from_others(chip, other, at):
        far, near = chip[:, at].astype(F32), other[:, at].astype(F32)
        low, high = jnp.where(core == 0, far, near), jnp.where(core == 0, near, far)
        return jnp.concatenate([low, high], axis=0)

    for h in range(GROUP):
        at = pl.ds(h * HEAD, HEAD)
        q = q_ref[:, at]
        ga = ga_ref[:, at]
        dots = jnp.sum(ga.astype(F32) * a_ref[:, at].astype(F32), axis=-1, keepdims=True)
        p = p_ref[h]
        ds = (p.astype(F32) * (dot_nt(ga, v_ref[:, at]) - dots)).astype(BF16)
        dsh = dsh_ref[h].astype(F32)
        dq = dot_nn(ds, k_ref[:, at])
        dq += dot_nn(jnp.where(facing, dsh, 0.0).astype(BF16), kl_ref[:, at])
        dq += dot_nn(jnp.where(facing, 0.0, dsh).astype(BF16), kr_ref[:, at])
        dq_ref[:, at] = (dq * SCALE).astype(BF16)
        dk_ref[:, at] = (dot_tn(ds, q) * SCALE + from_others(chip_k, core_k, at)).astype(BF16)
        dv_ref[:, at] = (dot_tn(p, ga) + from_others(chip_v, core_v, at)).astype(BF16)


def main_backward(
    ga, att, q, k, v, halo_chip, halo_core, probs, ds_halo, from_chip, from_core, after
):
    rows, feats = q.shape
    groups, col, hk, hv, own, halo = attention_specs(rows, feats)
    return run(
        main_backward_kernel,
        (ga, att, q, k, v, halo_chip, halo_core, probs, ds_halo)
        + (from_chip, from_chip, from_core, from_core),
        [col, col, col, col, col, hk, hk, own, halo, hk, hv, hk, hv],
        [col, col, col],
        [shape((rows, feats))] * 3,
        "main_backward",
        after,
        (groups,),
    )


def first_sends_kernel(k_ref, v_ref, w_ref, c_ref, chip_ref, core_ref, shard_ref, half_ref, held, sems):
    y, core = place()
    rows, feats = k_ref.shape
    step = 48
    copies = []
    for i, source in enumerate((k_ref, v_ref)):
        for j in range(0, rows, step):
            at = pl.ds(j, step)
            copies.append((source.at[at], held.at[i, at]))
    copies.append((w_ref, shard_ref))
    for j in range(0, rows, step):
        at = pl.ds(j, step)
        copies.append((c_ref.at[at, columns((1 - y) * feats, feats)], half_ref.at[at]))
    copies = [pltpu.make_async_copy(*ends, sems.at[i]) for i, ends in enumerate(copies)]
    for copy in copies:
        copy.start()
    for copy in copies:
        copy.wait()
    for i in range(2):
        at = pl.ds(i * feats, feats)
        low, high = held[i, :TILE], held[i, rows - TILE :]
        chip_ref[:, at] = jnp.where(core == 0, low, high)
        core_ref[:, at] = jnp.where(core == 0, high, low)


def first_sends(k, v, w, cot):
    rows, feats = k.shape
    return run(
        first_sends_kernel,
        (k, v, w, cot),
        [pl.BlockSpec(memory_space=pltpu.HBM)] * 4,
        [whole()] * 4,
        [shape((TILE, 2 * feats))] * 2 + [shape(w.shape), shape((rows, cot.shape[1] // 2))],
        "first_sends",
        limit=FIRST,
        scratch_shapes=[pltpu.VMEM((2, rows, feats), BF16), pltpu.SemaphoreType.DMA((16,))],
    )


def core_sends_kernel(cot_ref, partner_ref, att_ref, w_ref, out_ref, att_out, w_out):
    y, core = place()
    rows, width = out_ref.shape[0] // 2, out_ref.shape[1]
    out_ref[:rows] = cot_ref[:, columns((2 * y + 1 - core) * width, width)]
    out_ref[rows:] = partner_ref[:, columns((1 - core) * width, width)]
    att_out[...] = att_ref[...]
    w_out[...] = w_ref[...]


def core_sends(cot, cot_partner, att, shard, after):
    rows, model = cot.shape
    return run(
        core_sends_kernel,
        (cot, cot_partner, att, shard),
        [whole()] * 4,
        [whole()] * 3,
        [shape((2 * rows, model // 4)), shape(att.shape), shape(shard.shape)],
        "core_sends",
        after,
    )


def block_at(shift):
    if not is_grid():
        return shift
    return lax.rem(lax.div(lax.axis_index("dp"), 2) + 4 - shift, 4)


def lay(pair, block):
    x = lax.rem(lax.axis_index("dp"), 2) if is_grid() else 0
    rows = pair[0].shape[0]
    block[rows_at(x * rows, rows), :] = pair[0][...]
    block[rows_at((1 - x) * rows, rows), :] = pair[1][...]


def half_product(c_ref, w_own, w_other, out_ref, sliced):
    y, core = place()
    half = y if sliced else 0
    width = w_own.shape[1]
    total = dot_nt(c_ref[:, columns((2 * half + core) * width, width)], w_own[...])
    total += dot_nt(c_ref[:, columns((2 * half + 1 - core) * width, width)], w_other[...])
    out_ref[...] = total.astype(out_ref.dtype)


def near_kernel(c_ref, w_own, w_other, out_ref, *, sliced):
    half_product(c_ref, w_own, w_other, out_ref, sliced)


def far_kernel(c_ref, own0, own1, other0, other1, out_ref, w_own, w_other, *, sliced):
    lay((own0, own1), w_own)
    lay((other0, other1), w_other)
    half_product(c_ref, w_own, w_other, out_ref, sliced)


def grad_attention_near(cot, near, dtype, sliced, after):
    rows = cot.shape[0]
    return run(
        functools.partial(near_kernel, sliced=sliced),
        (cot, *near),
        [whole()] * 3,
        whole(),
        shape((rows, near[0].shape[0]), dtype),
        "grad_attention_near",
        after,
    )


def grad_attention_far(cot, far, dtype, sliced, after):
    rows = cot.shape[0]
    feats, width = 2 * far[0].shape[0], far[0].shape[1]
    return run(
        functools.partial(far_kernel, sliced=sliced),
        (cot, *far),
        [whole()] * 5,
        whole(),
        shape((rows, feats), dtype),
        "grad_attention_far",
        after,
        scratch_shapes=[pltpu.VMEM((feats, width), BF16)] * 2,
    )


def merge_kernel(own_near, own_far, recv_near, recv_far, out_ref):
    rows, width = own_far.shape
    for i, shift in enumerate((*NEAR, FAR)):
        own, recv = (own_near, recv_near) if i < 3 else (own_far, recv_far)
        at = pl.ds(i * width if i < 3 else 0, width)
        total = own[:, at].astype(F32) + recv[:, at].astype(F32)
        out_ref[:, columns(block_at(shift) * width, width)] = total.astype(BF16)


def merge(own_near, own_far, recv_near, recv_far, after):
    rows, width = own_far.shape
    return run(
        merge_kernel,
        (own_near, own_far, recv_near, recv_far),
        [whole()] * 4,
        whole(),
        shape((rows, 4 * width)),
        "merge",
        after,
    )


def project_kernel(
    a_own, a_par, near_own, near_other, own0, own1, other0, other1, mine, theirs, far_own, far_other
):
    y, core = place()
    rows, width = far_own.shape
    lay((own0, own1), far_own)
    lay((other0, other1), far_other)
    for quarter, near, far in ((core, near_own, far_own), (1 - core, near_other, far_other)):
        for a_ref, out_ref in ((a_par, theirs), (a_own, mine)):
            total = dot_nn(a_ref[:, columns(block_at(FAR) * rows, rows)], far[...])
            for i, shift in enumerate(NEAR):
                a = a_ref[:, columns(block_at(shift) * rows, rows)]
                total += dot_nn(a, near[i * rows : (i + 1) * rows])
            out_ref[:, columns(quarter * width, width)] = total.astype(BF16)


def project_half(att, att_partner, near, far, after):
    rows, feats = att.shape
    feats, width = 2 * far[0].shape[0], far[0].shape[1]
    return run(
        project_kernel,
        (att, att_partner, *near, *far),
        [whole()] * 8,
        [whole()] * 2,
        [shape((rows, 2 * width))] * 2,
        "project_half",
        after,
        scratch_shapes=[pltpu.VMEM((feats, width), BF16)] * 2,
    )


def join_halves_kernel(mine, theirs, out_ref):
    y, core = place()
    width = mine.shape[1]
    out_ref[:, columns(y * width, width)] = mine[...]
    out_ref[:, columns((1 - y) * width, width)] = theirs[...]


def join_halves(mine, theirs):
    rows, width = mine.shape
    return run(
        join_halves_kernel,
        (mine, theirs),
        [whole()] * 2,
        whole(),
        shape((rows, 2 * width)),
        "join_halves",
    )


def assemble_kernel(*refs):
    *pieces, out, sems = refs
    x = lax.rem(lax.axis_index("dp"), 2)
    rows = pieces[0].shape[0]
    copies = []
    for i, piece in enumerate(pieces):
        block = 2 * (i // 2) + (x if i % 2 == 0 else 1 - x)
        copies.append(pltpu.make_async_copy(piece, out.at[rows_at(block * rows, rows)], sems.at[i]))
    for copy in copies:
        copy.start()
    for copy in copies:
        copy.wait()


def assemble(pieces, after):
    rows, width = pieces[0].shape
    n = len(pieces)
    return run(
        assemble_kernel,
        pieces,
        [anywhere()] * n,
        whole(),
        shape((n * rows, width)),
        "assemble_weight",
        after,
        scratch_shapes=[pltpu.SemaphoreType.DMA((n,))],
    )


def along_z(block, shift):
    return lax.ppermute(
        block, "dp", [(2 * z + x, 2 * ((z + shift) % 4) + x) for z in range(4) for x in range(2)]
    )


def across_x(block):
    return lax.ppermute(block, "dp", [(i, i ^ 1) for i in range(8)])


def is_grid():
    return lax.axis_size("dp") == 8


def weight_grad_kernel(
    a_own, a_par, a_sib, a_sibpar, c_own, c_par, c_sib, c_sibpar, *outs_and_total
):
    *outs, total = outs_and_total
    x = lax.rem(lax.axis_index("dp"), 2)
    step = pl.program_id(0)
    half = total.shape[0] // 2
    acc = dot_tn(a_own[...], c_own[...])
    acc += dot_tn(a_par[...], c_par[...])
    acc += dot_tn(a_sib[...], c_sib[...])
    acc += dot_tn(a_sibpar[...], c_sibpar[...])
    total[...] = acc
    keep, *sends = outs
    keep[...] = total[rows_at(x * half, half), :].astype(BF16)
    for at, (part, row) in enumerate(((0, 0), (1, 0), (1, half), (2, 0))):

        @pl.when(step == at)
        def _():
            sends[part][row : row + half] = total[rows_at((1 - x) * half, half), :].astype(BF16)


def weight_grad_parts(operands, after):
    a_own, a_par, a_sib, a_sibpar, cot, cot_par, c_sib = operands
    tokens, feats = a_own.shape
    width = cot.shape[1] // 4
    part = feats // 4

    def rows_of(g):
        shift = jnp.where(g == 0, 2, jnp.where(g == 1, 1, jnp.where(g == 2, 3, 0)))
        return lax.rem(lax.div(lax.axis_index("dp"), 2) + shift, 4)

    a_spec = pl.BlockSpec((tokens, part), lambda g: (0, rows_of(g)))
    c_specs = [
        pl.BlockSpec((tokens, width), lambda g: (0, lax.axis_index("tile"))),
        pl.BlockSpec((tokens, width), lambda g: (0, lax.rem(lax.axis_index("tile"), 2))),
        pl.BlockSpec((tokens, width), lambda g: (0, 0)),
        pl.BlockSpec((tokens, width), lambda g: (1, 0)),
    ]
    dims = [(part // 2, width), (part, width), (part // 2, width)]
    return run(
        weight_grad_kernel,
        (a_own, a_par, a_sib, a_sibpar, cot, cot_par, c_sib, c_sib),
        [a_spec] * 4 + c_specs,
        [pl.BlockSpec((part // 2, width), lambda g: (g, 0))]
        + [pl.BlockSpec(d, lambda g: (0, 0)) for d in dims],
        [shape((2 * part, width))] + [shape(d) for d in dims],
        "weight_grad_parts",
        after,
        (4,),
        scratch_shapes=[pltpu.VMEM((part, width), F32)],
    )


def weight_grad_sum(operands, after):
    if not is_grid():
        a_own, a_par, a_sib, a_sibpar, cot, cot_par, c_sib = operands
        y, core = place()
        tokens, width = c_sib.shape[0] // 2, c_sib.shape[1]
        c_own = lax.dynamic_slice_in_dim(cot, (2 * y + core) * width, width, axis=1)
        c_par = lax.dynamic_slice_in_dim(cot_par, core * width, width, axis=1)
        total = dot_tn(a_own, c_own) + dot_tn(a_par, c_par)
        total += dot_tn(a_sib, c_sib[:tokens]) + dot_tn(a_sibpar, c_sib[tokens:])
        return lax.psum_scatter(total, "dp", scatter_dimension=0, tiled=True)
    parts = weight_grad_parts(operands, after)
    return parts[0], across_x(parts[1]), across_x(parts[2]), parts[3]


def kept(keep, slot):
    rows, width = keep.shape
    return pl.BlockSpec((rows // 4, width), lambda g: (slot, 0))


def one_step(block):
    return pl.BlockSpec(block.shape, lambda g: (0, 0))


def add_kernel(*refs):
    *terms, out = refs
    total = terms[0][...].astype(F32)
    for term in terms[1:]:
        total += term[...].astype(F32)
    out[...] = total.astype(out.dtype)


def add(first, spec, terms, dtype, after=()):
    return run(
        add_kernel,
        (first, *terms),
        [spec] + [one_step(term) for term in terms],
        one_step(terms[0]),
        shape(terms[0].shape, dtype),
        "add",
        after,
        (1,),
    )


def middle_sums_kernel(keep_one, keep_three, recv, from_two, one, three):
    half = one.shape[0]
    total = keep_one[...].astype(F32) + recv[:half].astype(F32) + from_two[...].astype(F32)
    one[...] = total.astype(BF16)
    three[...] = (keep_three[...].astype(F32) + recv[half:].astype(F32)).astype(BF16)


def middle_sums(keep, recv, from_two, after):
    return run(
        middle_sums_kernel,
        (keep, keep, recv, from_two),
        [kept(keep, 1), kept(keep, 2), one_step(recv), one_step(from_two)],
        [one_step(from_two)] * 2,
        [shape(from_two.shape)] * 2,
        "middle_sums",
        after,
        (1,),
    )


def between_chips(block):
    return lax.ppermute(block, "tile", [(1, 2), (2, 1)])


def to_partner(block):
    return lax.ppermute(block, "tile", [(0, 2), (1, 3), (2, 0), (3, 1)])


def to_core(block):
    return lax.ppermute(block, "tile", [(0, 1), (1, 0), (2, 3), (3, 2)])


def shards(queries, key_vectors, value_vectors, out_weight, cotangent):
    q, k, v, cot = queries[0], key_vectors[0], value_vectors[0], cotangent[0]
    tokens = q.shape[0]
    y, core = place()

    rim_chip, rim_core, shard, cot_send = first_sends(k, v, out_weight, cot)
    halo_chip, halo_core = between_chips(rim_chip), to_core(rim_core)
    if is_grid():
        z1, z3 = along_z(shard, 1), along_z(shard, 3)
        x0 = across_x(shard)
    cot_partner = to_partner(cot_send)
    att, probs, probs_halo = attention_forward(q, k, v, halo_chip, halo_core, (z1, z3) if is_grid() else ())
    att_partner = to_partner(att)
    if is_grid():
        x1, x3 = across_x(z1), across_x(z3)
        z2 = relay(along_z(z1, 1), (att,))
        near_own = assemble((shard, x0, z1, x1, z3, x3), (att, cot_partner))
        far_own = (z2, across_x(z2))
    else:
        w_own = lax.all_gather(out_weight, "dp", axis=0, tiled=True)
        cut = w_own.shape[0] * 3 // 4
        near_own = w_own[:cut]
        far_own = (w_own[cut : cut + cut // 6], w_own[cut + cut // 6 :])
    near = (near_own, to_core(near_own))
    cot_send_core, att_send, far_send = core_sends(cot, cot_partner, att, far_own[0], (near_own,))
    cot_core, att_core = to_core(cot_send_core), to_core(att_send)
    far = (*far_own, to_core(far_send), to_core(far_own[1]))

    send_near = grad_attention_near(cot_partner, near, BF16, False, (cot_send_core,))
    recv_near = to_partner(send_near)
    send_far = grad_attention_far(cot_partner, far, BF16, False, (send_near,))
    recv_far = to_partner(send_far)

    att_partner = relay(att_partner, (send_far,))
    att_core_partner = to_core(att_partner)
    mine_near = grad_attention_near(cot, near, BF16, True, (send_far,))
    parts = weight_grad_sum(
        (att, att_partner, att_core, att_core_partner, cot, cot_partner, cot_core), (mine_near,)
    )
    grid = is_grid()
    mine_far = grad_attention_far(
        cot, far, BF16, True, (mine_near, parts[0]) if grid else (mine_near,)
    )
    proj_own, proj_partner = project_half(att, att_partner, near, far, (mine_far,))
    proj_recv = to_partner(proj_partner)
    if grid:
        far_sum = add(parts[0], kept(parts[0], 0), (parts[1],), BF16, (proj_partner,))
        from_two = along_z(far_sum, 1)
        recv = across_x(relay(parts[3], (far_sum,)))

    ga = merge(mine_near, mine_far, recv_near, recv_far, (far_sum,) if grid else ())
    ds_halo, back_chip, back_core = halo_backward(ga, att, q, halo_chip, halo_core, probs_halo)
    from_chip, from_core = between_chips(back_chip), to_core(back_core)
    if grid:
        one, three = middle_sums(parts[0], parts[2], from_two, (ds_halo,))
        from_one, from_three = along_z(one, 1), along_z(three, 3)
    dq, dk, dv = main_backward(
        ga, att, q, k, v, halo_chip, halo_core, probs, ds_halo, from_chip, from_core, (one,) if grid else ()
    )
    projected = join_halves(proj_own, proj_recv)
    weight_grad = parts
    if grid:
        near_sum = add(parts[0], kept(parts[0], 3), (recv, from_three), F32, (dq,))
        weight_grad = add(near_sum, one_step(near_sum), (from_one,), F32)
    return projected[None], dq[None], dk[None], dv[None], weight_grad


def solution(mesh):
    tokens = P("dp", "tile", None)
    weight = P("dp", "tile")
    return jax.shard_map(
        shards,
        mesh=mesh,
        in_specs=(tokens, tokens, tokens, weight, tokens),
        out_specs=(tokens, tokens, tokens, tokens, weight),
        check_vma=False,
    )
```
